32 devices in a mesh: dp: 8 (over z, y), ctx: 4 (over x, core).
Axes of the slice: x: 2, y: 2, z: 4, core: 2. Of those that a mesh axis runs over, the one named last changes fastest.
Arguments:
- qkvu: bfloat16 [4096, 2048], P(('dp', 'ctx')), may hold values from -6 to 6
- actions: int32 [4096], P(('dp', 'ctx')), may hold values from 0 to 63
- lengths: int32 [8, 4], P('dp'), may hold values from 1 to 448, 512 in all within a row
- action_table: bfloat16 [64, 512], replicated, may hold values from -6 to 6
- gain: float32 [512], replicated, may hold values from 0.1 to 1.9
- w_out: bfloat16 [512, 1024], replicated, may hold values from -0.25 to 0.25
- cotangent: bfloat16 [4096, 1024], P(('dp', 'ctx')), may hold values from -6 to 6
Outputs:
- output: bfloat16 [4096, 1024], P(('dp', 'ctx'))
- d_qkvu: bfloat16 [4096, 2048], P(('dp', 'ctx'))
- d_wout: float32 [512, 1024], P('dp')
- d_table: float32 [64, 512], replicated
- d_gain: float32 [512], replicated
The draws below stay inside these ranges and needn't reach their ends.
Inputs may be any that keep to these rules, and one draw needn't show every extreme that they name: Each row holds the lengths of the 4 histories packed in row order into one group's 512 rows; they sum to 512.
All inputs are finite; a program needn't handle non-finite values.
Results may differ from the reference program's by a relative error of at most 0.0066.
Values may be sent and summed in bfloat16 or wider, within the bound.
A program may use at most 64 MiB of HBM per device.

```python
import math
import jax
import jax.numpy as jnp
import numpy as np
from jax import lax

D = 1024
HEADS = 4
HD = 128
ACTIONS = 64
SEQS = 4
HV = 512
PACK = 512
MOST = 448
TOKENS = 4096
N_DP = 8


def plant(array, own_key, smallest, largest):
    dims = array.shape
    spot = [jax.random.randint(jax.random.fold_in(own_key, axis), (), 0, dims[axis]) for axis in range(len(dims))]
    array = array.at[tuple(spot)].set(smallest)
    longest = dims.index(max(dims))
    spot[longest] = (spot[longest] + 1) % dims[longest]
    return array.at[tuple(spot)].set(largest)


def block_scale(rng, extent, pieces, low, high):
    level, own = 1.0, jax.random.fold_in(rng, 6)
    for position, parts in pieces:
        heights = jnp.exp(jax.random.uniform(jax.random.fold_in(own, position), (parts,), jnp.float32, low / len(pieces), high / len(pieces)))
        level = level * jnp.repeat(heights, extent[position] // parts).reshape([-1 if axis == position else 1 for axis in range(len(extent))])
    return level


def rank_table(amount, lean):
    portions = [(1 << 20) // math.isqrt(standing ** lean) + 1 for standing in range(1, amount + 1)]
    width = 1 + sum(portions) // (1 << 30)
    return np.cumsum(np.array([max(1, weight // width) for weight in portions]))


def ranked_ids(stream_key, extent, amount, lean):
    grid = rank_table(amount, lean)
    lot = jax.random.randint(jax.random.fold_in(stream_key, 1), extent, 0, int(grid[amount - 1]))
    rank = jnp.searchsorted(jnp.asarray(grid, jnp.int32), lot, side="right")
    return jax.random.permutation(jax.random.fold_in(stream_key, 2), amount)[rank].astype(jnp.int32)


def profile(number_of, total, reach, slope):
    loads = [(1 << 20) // math.isqrt(rank ** slope) + 1 for rank in range(2, number_of + 1)]
    rest, counts = total - reach - (number_of - 1), [1] * (number_of - 1)
    while rest > 0:
        candidates = [i for i in range(number_of - 1) if counts[i] < reach]
        pool, budget = sum([loads[i] for i in candidates]), rest
        for i in candidates:
            more = min(reach - counts[i], max(1, budget * loads[i] // pool), rest)
            counts[i] = counts[i] + more
            rest = rest - more
    return np.array([reach] + counts)


def uneven(rng, amount, total, limit, slope):
    if amount == 2:
        one = jax.random.randint(rng, (), max(1, total - limit), min(limit, total - 1) + 1)
        return jnp.stack([one, total - one])
    sizes = jnp.asarray(profile(amount, total, limit, slope), jnp.int32)
    twos = (amount - 1) // 2
    donor, receiver = sizes[1:1 + 2 * twos:2], sizes[2:2 + 2 * twos:2]
    margin = jnp.minimum(donor - 1, limit - receiver)
    shifted = jax.random.randint(jax.random.fold_in(rng, 1), (twos,), 0, 1 << 20) % (margin + 1)
    sizes = sizes.at[1:1 + 2 * twos:2].set(donor - shifted).at[2:2 + 2 * twos:2].set(receiver + shifted)
    return sizes[jax.random.permutation(jax.random.fold_in(rng, 2), amount)]


def normal_values(own_key, dims, spread, limit, cuts=(), kind=jnp.bfloat16):
    factor_of = block_scale(own_key, dims, cuts, -0.22, 0.18) if cuts else 1.0
    result = jax.random.normal(own_key, dims, jnp.float32) * spread * factor_of
    return jnp.minimum(jnp.maximum(result, -limit), limit).astype(kind)


def setup_inputs(seed: int = 0) -> dict:
    splits = jax.random.split(jax.random.key(seed), 8)
    return {
        "qkvu": normal_values(splits[0], (TOKENS, 4 * HV), 1.0, 6.0, ((0, 32),)),
        "actions": plant(ranked_ids(splits[1], (TOKENS,), ACTIONS, 2), jax.random.fold_in(splits[1], 3), 0, ACTIONS - 1).astype(jnp.int32),
        "lengths": jax.vmap(lambda own: uneven(own, SEQS, PACK, MOST, 2))(jax.random.split(splits[2], N_DP)).reshape((N_DP, SEQS)).astype(jnp.int32),
        "action_table": normal_values(splits[3], (ACTIONS, HV), 1.0, 6.0),
        "gain": jnp.clip(1.0 + 0.18 * jax.random.normal(splits[4], (HV,), jnp.float32), 0.1, 1.9),
        "w_out": normal_values(splits[5], (HV, D), HV ** -0.5, 0.25),
        "cotangent": normal_values(splits[6], (TOKENS, D), 1.0, 6.0, ((0, 32),)),
    }


def silu_slope(inputs):
    sig = jax.nn.sigmoid(inputs)
    return sig * (1.0 + inputs * (1.0 - sig))

def history_of(positions, lengths_row):
    boundary = jnp.cumsum(lengths_row).astype(jnp.int32)
    history = lax.optimization_barrier(jnp.sum((positions[:, None] >= boundary[None, :]).astype(jnp.int32), axis=1))
    member = history[:, None] == jnp.arange(lengths_row.shape[0], dtype=jnp.int32)[None, :]
    seq_length = lax.optimization_barrier(jnp.sum(jnp.where(member, lengths_row[None, :], 0), axis=1)).astype(jnp.float32)
    return (history, seq_length)

def one_group(packed):
    qkvu_rows, action_rows, lengths_row, cotangent_rows, action_table, gain, w_out = packed
    scale = HD ** (-0.5)
    positions = jnp.arange(PACK, dtype=jnp.int32)
    history, seq_length = history_of(positions, lengths_row)
    allowed = (history[:, None] == history[None, :]) & (positions[None, :] <= positions[:, None])
    raw = qkvu_rows.astype(jnp.float32)
    onehot = (action_rows[:, None] == jnp.arange(ACTIONS, dtype=jnp.int32)[None, :]).astype(jnp.bfloat16)
    embedded = jnp.dot(onehot, action_table, preferred_element_type=jnp.float32)
    gate_pre = raw[:, :HV] + embedded
    gate = jax.nn.silu(gate_pre)
    value_pre = raw[:, HV:2 * HV]
    query_pre = raw[:, 2 * HV:3 * HV]
    key_pre = raw[:, 3 * HV:]
    vals = jax.nn.silu(value_pre).astype(jnp.bfloat16).reshape(PACK, HEADS, HD).astype(jnp.float32)
    queries = jax.nn.silu(query_pre).astype(jnp.bfloat16).reshape(PACK, HEADS, HD).astype(jnp.float32)
    keys = jax.nn.silu(key_pre).astype(jnp.bfloat16).reshape(PACK, HEADS, HD).astype(jnp.float32)
    scores = jnp.einsum('qhd,khd->hqk', queries, keys) * scale
    weights = jnp.where(allowed[None], jax.nn.silu(scores) / seq_length[None, :, None], 0.0).astype(jnp.bfloat16).astype(jnp.float32)
    attended = jnp.einsum('hqk,khd->qhd', weights, vals).reshape(PACK, HV)
    centre = attended - lax.optimization_barrier(jnp.mean(attended, axis=1, keepdims=True))
    inv_std = lax.rsqrt(lax.optimization_barrier(jnp.mean(centre * centre, axis=1, keepdims=True)) + 1e-05)
    normed = centre * inv_std
    mixed = (normed * gain * gate).astype(jnp.bfloat16)
    output = jnp.dot(mixed, w_out, preferred_element_type=jnp.float32).astype(jnp.bfloat16)
    grad_mixed = jnp.dot(cotangent_rows, w_out.T, preferred_element_type=jnp.float32)
    weight_term = jnp.dot(mixed.T, cotangent_rows, preferred_element_type=jnp.float32)
    gain_term = lax.optimization_barrier(jnp.sum(grad_mixed * normed * gate, axis=0))
    grad_gate = grad_mixed * gain * normed * silu_slope(gate_pre)
    table_term = jnp.dot(onehot.astype(jnp.float32).T, grad_gate, precision=lax.Precision.HIGHEST)
    pushed = grad_mixed * gain * gate
    grad_out = ((pushed - lax.optimization_barrier(jnp.mean(pushed, axis=1, keepdims=True)) - normed * lax.optimization_barrier(jnp.mean(pushed * normed, axis=1, keepdims=True))) * inv_std).astype(jnp.bfloat16)
    grad_heads = grad_out.reshape(PACK, HEADS, HD).astype(jnp.float32)
    grad_prod = jnp.einsum('qhd,khd->hqk', grad_heads, vals)
    grad_scores = jnp.where(allowed[None], grad_prod * silu_slope(scores) / seq_length[None, :, None], 0.0).astype(jnp.bfloat16).astype(jnp.float32)
    grad_query = jnp.einsum('hqk,khd->qhd', grad_scores, keys).reshape(PACK, HV) * scale
    grad_key = jnp.einsum('hqk,qhd->khd', grad_scores, queries).reshape(PACK, HV) * scale
    grad_value = jnp.einsum('hqk,qhd->khd', weights, grad_heads).reshape(PACK, HV)
    d_rows = jnp.concatenate([grad_gate, grad_value * silu_slope(value_pre), grad_query * silu_slope(query_pre), grad_key * silu_slope(key_pre)], axis=1).astype(jnp.bfloat16)
    return (output, d_rows, weight_term, table_term, gain_term)

def reference(qkvu, actions, lengths, action_table, gain, w_out, cotangent):
    groups = qkvu.shape[0] // PACK
    qkvu_groups = qkvu.reshape(groups, PACK, 4 * HV)
    action_groups = actions.reshape(groups, PACK)
    cotangent_groups = cotangent.reshape(groups, PACK, D)

    def apply_group(packed):
        qkvu_rows, action_rows, lengths_row, cotangent_rows = packed
        return one_group((qkvu_rows, action_rows, lengths_row, cotangent_rows, action_table, gain, w_out))
    output, d_rows, weight_terms, table_terms, gain_terms = lax.map(apply_group, (qkvu_groups, action_groups, lengths, cotangent_groups))
    output = output.reshape(groups * PACK, D)
    d_qkvu = d_rows.reshape(groups * PACK, 4 * HV)
    return (output, d_qkvu, lax.optimization_barrier(jnp.sum(weight_terms, axis=0)), lax.optimization_barrier(jnp.sum(table_terms, axis=0)), lax.optimization_barrier(jnp.sum(gain_terms, axis=0)))
```

```python
import functools

import jax
import jax.numpy as jnp
from jax import lax
from jax.experimental import pallas as pl
from jax.experimental.pallas import tpu as pltpu
from jax.sharding import PartitionSpec as P

HD = 128
ACTIONS = 64
F32 = jnp.float32
BF16 = jnp.bfloat16
CTX_KINDS = ("kv", "q", "cot", "mix", "dout", "tab", "gain", "wfin", "tfin")
DP_KINDS = ("wdp", "tdp", "gdp")


def sigmoid(x):
    return 0.5 * jnp.tanh(0.5 * x) + 0.5


def silu_slope(x):
    sig = sigmoid(x)
    return sig * (1.0 + x * (1.0 - sig))


def dot_nn(a, b):
    return lax.dot_general(a, b, (((1,), (0,)), ((), ())), preferred_element_type=F32)


def dot_nt(a, b):
    return lax.dot_general(a, b, (((1,), (1,)), ((), ())), preferred_element_type=F32)


def dot_tn(a, b):
    return lax.dot_general(a, b, (((0,), (0,)), ((), ())), preferred_element_type=F32)


def layer_kernel(
    n_ctx, n_dp, f_parts,
    qkvu_ref, act_ref, len_ref, table_ref, gain_ref, wout_ref, cot_ref,
    out_ref, dqkvu_ref, dwout_ref, dtable_ref, dgain_ref,
    kv_buf, q_buf, cot_buf, mix_buf, do_buf, tab_src, tab_buf, gain_buf,
    wdp_src, wdp_buf, tdp_src, tdp_buf, gdp_src, gdp_buf, wfin_buf, tfin_buf,
    p_q, w_k, p_k, acc, acc_k, acc_v, gm_ref, gate_ref, gslope_ref,
    ctx_send, ctx_recv, dp_send, dp_recv,
):
    me = lax.axis_index("ctx")
    dpi = lax.axis_index("dp")
    rows = qkvu_ref.shape[0]
    width = wout_ref.shape[0]
    heads = width // HD
    scale = HD ** (-0.5)
    c_width = cot_buf.shape[2]
    dp_rows = dwout_ref.shape[0]
    p_rows = dp_rows // f_parts
    t_rows = tab_buf.shape[1]

    def ctx_copy(kind, src, dst, peer):
        k = CTX_KINDS.index(kind)
        return pltpu.make_async_remote_copy(
            src_ref=src, dst_ref=dst,
            send_sem=ctx_send.at[k, peer], recv_sem=ctx_recv.at[k, me],
            device_id={"ctx": peer}, device_id_type=pl.DeviceIdType.MESH,
        )

    def ctx_arrived(kind, buf, source):
        k = CTX_KINDS.index(kind)
        pltpu.make_async_remote_copy(
            src_ref=buf.at[source], dst_ref=buf.at[source],
            send_sem=ctx_send.at[k, source], recv_sem=ctx_recv.at[k, source],
            device_id={"ctx": source}, device_id_type=pl.DeviceIdType.MESH,
        ).wait_recv()

    def dp_copy(kind, src, dst, peer):
        k = DP_KINDS.index(kind)
        return pltpu.make_async_remote_copy(
            src_ref=src, dst_ref=dst,
            send_sem=dp_send.at[k, peer], recv_sem=dp_recv.at[k, dpi],
            device_id={"dp": peer}, device_id_type=pl.DeviceIdType.MESH,
        )

    def dp_arrived(kind, buf, source):
        k = DP_KINDS.index(kind)
        pltpu.make_async_remote_copy(
            src_ref=buf.at[source], dst_ref=buf.at[source],
            send_sem=dp_send.at[k, source], recv_sem=dp_recv.at[k, source],
            device_id={"dp": source}, device_id_type=pl.DeviceIdType.MESH,
        ).wait_recv()

    def ctx_peer(d):
        return lax.rem(me + d, n_ctx)

    def dp_peer(d):
        return lax.rem(dpi + d, n_dp)

    barrier = pltpu.get_barrier_semaphore()
    for d in range(1, n_ctx):
        pl.semaphore_signal(
            barrier, inc=1, device_id={"ctx": ctx_peer(d)}, device_id_type=pl.DeviceIdType.MESH
        )
    for d in range(1, n_dp):
        pl.semaphore_signal(
            barrier, inc=1, device_id={"dp": dp_peer(d)}, device_id_type=pl.DeviceIdType.MESH
        )

    def activated(block):
        x = qkvu_ref[:, block * width : (block + 1) * width].astype(F32)
        return (x * sigmoid(x)).astype(BF16)

    kv_buf[me, :, :width] = activated(3)
    kv_buf[me, :, width:] = activated(1)
    q_buf[me] = activated(2)
    pl.semaphore_wait(barrier, n_ctx - 1 + n_dp - 1)

    def kv_copy(peer):
        return ctx_copy("kv", kv_buf.at[me], kv_buf.at[me], peer)

    def q_copy(peer):
        return ctx_copy("q", q_buf.at[me], q_buf.at[me], peer)

    def do_copy(peer):
        return ctx_copy("dout", do_buf.at[me], do_buf.at[me], peer)

    def cot_copy(peer):
        start = pl.multiple_of((peer // f_parts) * c_width, c_width)
        return ctx_copy("cot", cot_ref.at[:, pl.ds(start, c_width)], cot_buf.at[me], peer)

    def mix_copy(peer):
        return ctx_copy("mix", mix_buf.at[me], mix_buf.at[me], peer)

    def tab_copy(peer):
        return ctx_copy("tab", tab_src.at[peer], tab_buf.at[me], peer)

    def gain_copy(peer):
        return ctx_copy("gain", gain_buf.at[me], gain_buf.at[me], peer)

    def wfin_copy(peer):
        return ctx_copy("wfin", wfin_buf.at[me], wfin_buf.at[me], peer)

    def tfin_copy(peer):
        return ctx_copy("tfin", tfin_buf.at[me], tfin_buf.at[me], peer)

    part = lax.rem(me, f_parts)

    def wdp_copy(peer):
        start = pl.multiple_of(peer * dp_rows + part * p_rows, p_rows)
        return dp_copy("wdp", wdp_src.at[pl.ds(start, p_rows)], wdp_buf.at[dpi], peer)

    def tdp_copy(peer):
        return dp_copy("tdp", tdp_src, tdp_buf.at[dpi], peer)

    def gdp_copy(peer):
        return dp_copy("gdp", gdp_src, gdp_buf.at[dpi], peer)

    def for_higher(action):
        for d in range(1, n_ctx):
            @pl.when(me + d < n_ctx)
            def _():
                action(me + d)

    def for_lower(action):
        for d in range(1, n_ctx):
            @pl.when(me >= d)
            def _():
                action(me - d)

    def for_others(action):
        for d in range(1, n_ctx):
            action(ctx_peer(d))

    def for_dp_others(action):
        for d in range(1, n_dp):
            action(dp_peer(d))

    for_higher(lambda p: kv_copy(p).start())
    for_lower(lambda p: q_copy(p).start())
    for_others(lambda p: cot_copy(p).start())
    own_start = pl.multiple_of((me // f_parts) * c_width, c_width)
    cot_buf[me] = cot_ref[:, pl.ds(own_start, c_width)]

    def history(pos):
        bound = jnp.int32(0)
        start = jnp.zeros_like(pos)
        length = jnp.zeros_like(pos)
        for s in range(len_ref.shape[1]):
            here = pos >= bound
            start = jnp.where(here, bound, start)
            length = jnp.where(here, len_ref[0, s], length)
            bound = bound + len_ref[0, s]
        return start, length

    sub = lax.broadcasted_iota(jnp.int32, (rows, rows), 0)
    lane = lax.broadcasted_iota(jnp.int32, (rows, rows), 1)

    def score_parts(s):
        sig = sigmoid(s)
        t = s * sig
        return t, sig + t * (1.0 - sig)

    def key_side_block(i):
        pos_q = i * rows + lane
        pos_k = me * rows + sub
        start, length = history(pos_q)
        allowed = (pos_k >= start) & (pos_k <= pos_q)
        factor = jnp.where(allowed, 1.0 / length.astype(F32), 0.0)
        for h in range(heads):
            cols = slice(h * HD, (h + 1) * HD)
            t, slope = score_parts(dot_nt(kv_buf[me, :, cols], q_buf[i, :, cols]) * scale)
            w_k[i, h] = (t * factor).astype(BF16)
            p_k[i, h] = slope * factor

    onehot_t = (
        lax.broadcasted_iota(jnp.int32, (ACTIONS, rows), 0) == act_ref[...]
    ).astype(BF16)
    gate_pre = qkvu_ref[:, :width].astype(F32) + dot_tn(onehot_t, table_ref[...])
    gate_sig = sigmoid(gate_pre)
    gate_ref[...] = gate_pre * gate_sig
    gslope_ref[...] = gate_sig * (1.0 + gate_pre * (1.0 - gate_sig))
    gm_ref[...] = dot_nt(cot_ref[...], wout_ref[...])
    key_side_block(me)

    acc[...] = jnp.zeros_like(acc)

    def forward(step, carry):
        j = me - step

        @pl.when(step > 0)
        def _():
            ctx_arrived("kv", kv_buf, j)

        pos_q = me * rows + sub
        pos_k = j * rows + lane
        start, length = history(pos_q)
        allowed = (pos_k >= start) & (pos_k <= pos_q)
        factor = jnp.where(allowed, 1.0 / length.astype(F32), 0.0)
        for h in range(heads):
            cols = slice(h * HD, (h + 1) * HD)
            vcols = slice(width + h * HD, width + (h + 1) * HD)
            t, slope = score_parts(dot_nt(q_buf[me, :, cols], kv_buf[j, :, cols]) * scale)
            p_q[j, h] = slope * factor
            acc[:, cols] += dot_nn((t * factor).astype(BF16), kv_buf[j, :, vcols])
        return carry

    lax.fori_loop(0, me + 1, forward, 0)

    attended = acc[...]
    gain = gain_ref[...]
    gate = gate_ref[...]
    centre = attended - jnp.mean(attended, axis=1, keepdims=True)
    inv_std = lax.rsqrt(jnp.mean(centre * centre, axis=1, keepdims=True) + 1e-05)
    normed = centre * inv_std
    mixed = (normed * gain * gate).astype(BF16)
    mix_buf[me] = mixed
    for_others(lambda p: mix_copy(p).start())
    grad_mixed = gm_ref[...]
    gated = grad_mixed * gate
    pushed = gated * gain
    grad_out = (
        pushed
        - jnp.mean(pushed, axis=1, keepdims=True)
        - normed * jnp.mean(pushed * normed, axis=1, keepdims=True)
    ) * inv_std
    do_buf[me] = grad_out.astype(BF16)
    for_lower(lambda p: do_copy(p).start())
    gain_buf[me] = jnp.sum(gated * normed, axis=0, keepdims=True)
    for_others(lambda p: gain_copy(p).start())
    grad_gate = grad_mixed * gain * normed * gslope_ref[...]
    dqkvu_ref[:, :width] = grad_gate.astype(BF16)
    high = grad_gate.astype(BF16)
    low = (grad_gate - high.astype(F32)).astype(BF16)
    table_term = dot_nn(onehot_t, high) + dot_nn(onehot_t, low)
    for s in range(n_ctx):
        tab_src[s] = table_term[s * t_rows : (s + 1) * t_rows]
    for_others(lambda p: tab_copy(p).start())
    tab_buf[me] = tab_src[me]

    out_ref[...] = dot_nn(mixed, wout_ref[...]).astype(BF16)

    acc[...] = jnp.zeros_like(acc)

    def query_grad(step, carry):
        j = me - step
        for h in range(heads):
            cols = slice(h * HD, (h + 1) * HD)
            vcols = slice(width + h * HD, width + (h + 1) * HD)
            prod = dot_nt(do_buf[me, :, cols], kv_buf[j, :, vcols])
            acc[:, cols] += dot_nn((prod * p_q[j, h]).astype(BF16), kv_buf[j, :, cols])
        return carry

    lax.fori_loop(0, me + 1, query_grad, 0)
    q_pre = qkvu_ref[:, 2 * width : 3 * width].astype(F32)
    dqkvu_ref[:, 2 * width : 3 * width] = (acc[...] * scale * silu_slope(q_pre)).astype(BF16)

    for_others(lambda p: ctx_arrived("gain", gain_buf, p))
    gain_sum = gain_buf[0]
    for s in range(1, n_ctx):
        gain_sum = gain_sum + gain_buf[s]
    gdp_src[...] = gain_sum
    for_dp_others(lambda p: gdp_copy(p).start())
    gdp_buf[dpi] = gain_sum
    for_others(lambda p: ctx_arrived("tab", tab_buf, p))
    tab_sum = tab_buf[0]
    for s in range(1, n_ctx):
        tab_sum = tab_sum + tab_buf[s]
    tdp_src[...] = tab_sum.astype(tdp_src.dtype)
    for_dp_others(lambda p: tdp_copy(p).start())
    tdp_buf[dpi] = tab_sum.astype(tdp_src.dtype)

    def key_side(i, carry):
        ctx_arrived("q", q_buf, i)
        key_side_block(i)
        return carry

    lax.fori_loop(me + 1, n_ctx, key_side, 0)

    for_others(lambda p: ctx_arrived("cot", cot_buf, p))
    for_others(lambda p: ctx_arrived("mix", mix_buf, p))
    w_sum = dot_tn(
        mix_buf[...].reshape(n_ctx * rows, width), cot_buf[...].reshape(n_ctx * rows, c_width)
    )
    wdp_src[...] = w_sum.astype(wdp_src.dtype)
    for_dp_others(lambda p: wdp_copy(p).start())
    own_rows = pl.multiple_of(dpi * dp_rows + part * p_rows, p_rows)
    wdp_buf[dpi] = wdp_src[pl.ds(own_rows, p_rows)]

    acc_k[...] = jnp.zeros_like(acc_k)
    acc_v[...] = jnp.zeros_like(acc_v)

    def key_grad(i, carry):
        @pl.when(i > me)
        def _():
            ctx_arrived("dout", do_buf, i)

        for h in range(heads):
            cols = slice(h * HD, (h + 1) * HD)
            vcols = slice(width + h * HD, width + (h + 1) * HD)
            grads = do_buf[i, :, cols]
            prod = dot_nt(kv_buf[me, :, vcols], grads)
            acc_k[:, cols] += dot_nn((prod * p_k[i, h]).astype(BF16), q_buf[i, :, cols])
            acc_v[:, cols] += dot_nn(w_k[i, h], grads)
        return carry

    lax.fori_loop(me, n_ctx, key_grad, 0)
    v_pre = qkvu_ref[:, width : 2 * width].astype(F32)
    dqkvu_ref[:, width : 2 * width] = (acc_v[...] * silu_slope(v_pre)).astype(BF16)
    k_pre = qkvu_ref[:, 3 * width :].astype(F32)
    dqkvu_ref[:, 3 * width :] = (acc_k[...] * scale * silu_slope(k_pre)).astype(BF16)

    for_dp_others(lambda p: dp_arrived("tdp", tdp_buf, p))
    total = tdp_buf[0].astype(F32)
    for s in range(1, n_dp):
        total = total + tdp_buf[s].astype(F32)
    tfin_buf[me] = total
    for_others(lambda p: tfin_copy(p).start())
    for_dp_others(lambda p: dp_arrived("gdp", gdp_buf, p))
    total = gdp_buf[0]
    for s in range(1, n_dp):
        total = total + gdp_buf[s]
    dgain_ref[...] = total
    for_dp_others(lambda p: dp_arrived("wdp", wdp_buf, p))
    total = wdp_buf[0].astype(F32)
    for s in range(1, n_dp):
        total = total + wdp_buf[s].astype(F32)
    wfin_buf[me] = total.astype(wfin_buf.dtype)
    for_others(lambda p: wfin_copy(p).start())
    for_others(lambda p: ctx_arrived("tfin", tfin_buf, p))
    for s in range(n_ctx):
        dtable_ref[s * t_rows : (s + 1) * t_rows] = tfin_buf[s]
    for_others(lambda p: ctx_arrived("wfin", wfin_buf, p))
    for s in range(n_ctx):
        top, left = (s % f_parts) * p_rows, (s // f_parts) * c_width
        dwout_ref[top : top + p_rows, left : left + c_width] = wfin_buf[s].astype(F32)

    for_higher(lambda p: kv_copy(p).wait_send())
    for_lower(lambda p: q_copy(p).wait_send())
    for_lower(lambda p: do_copy(p).wait_send())
    for copy in (cot_copy, mix_copy, tab_copy, gain_copy, wfin_copy, tfin_copy):
        for_others(lambda p: copy(p).wait_send())
    for copy in (wdp_copy, tdp_copy, gdp_copy):
        for_dp_others(lambda p: copy(p).wait_send())


def on_device(n_ctx, n_dp, qkvu, actions, lengths, action_table, gain, w_out, cotangent):
    rows = qkvu.shape[0]
    width, model = w_out.shape
    heads = width // HD
    c_parts = min(n_ctx, model // 128)
    f_parts = n_ctx // c_parts
    c_width = model // c_parts
    dp_rows = width // n_dp
    p_rows = dp_rows // f_parts
    t_rows = ACTIONS // n_ctx
    w_kind = BF16 if p_rows % 16 == 0 else F32
    t_kind = BF16 if t_rows % 16 == 0 else F32
    vmem = pl.BlockSpec(memory_space=pltpu.VMEM)
    outs = pl.pallas_call(
        functools.partial(layer_kernel, n_ctx, n_dp, f_parts),
        out_shape=(
            jax.ShapeDtypeStruct((rows, model), BF16),
            jax.ShapeDtypeStruct((rows, 4 * width), BF16),
            jax.ShapeDtypeStruct((dp_rows, model), F32),
            jax.ShapeDtypeStruct((ACTIONS, width), F32),
            jax.ShapeDtypeStruct((1, width), F32),
        ),
        in_specs=[vmem, vmem, pl.BlockSpec(memory_space=pltpu.SMEM), vmem, vmem, vmem, vmem],
        out_specs=(vmem,) * 5,
        scratch_shapes=[
            pltpu.VMEM((n_ctx, rows, 2 * width), BF16),
            pltpu.VMEM((n_ctx, rows, width), BF16),
            pltpu.VMEM((n_ctx, rows, c_width), BF16),
            pltpu.VMEM((n_ctx, rows, width), BF16),
            pltpu.VMEM((n_ctx, rows, width), BF16),
            pltpu.VMEM((n_ctx, t_rows, width), F32),
            pltpu.VMEM((n_ctx, t_rows, width), F32),
            pltpu.VMEM((n_ctx, 1, width), F32),
            pltpu.VMEM((width, c_width), w_kind),
            pltpu.VMEM((n_dp, p_rows, c_width), w_kind),
            pltpu.VMEM((t_rows, width), t_kind),
            pltpu.VMEM((n_dp, t_rows, width), t_kind),
            pltpu.VMEM((1, width), F32),
            pltpu.VMEM((n_dp, 1, width), F32),
            pltpu.VMEM((n_ctx, p_rows, c_width), w_kind),
            pltpu.VMEM((n_ctx, t_rows, width), F32),
            pltpu.VMEM((n_ctx, heads, rows, rows), F32),
            pltpu.VMEM((n_ctx, heads, rows, rows), BF16),
            pltpu.VMEM((n_ctx, heads, rows, rows), F32),
            pltpu.VMEM((rows, width), F32),
            pltpu.VMEM((rows, width), F32),
            pltpu.VMEM((rows, width), F32),
            pltpu.VMEM((rows, width), F32),
            pltpu.VMEM((rows, width), F32),
            pltpu.VMEM((rows, width), F32),
            pltpu.SemaphoreType.DMA((len(CTX_KINDS), n_ctx)),
            pltpu.SemaphoreType.DMA((len(CTX_KINDS), n_ctx)),
            pltpu.SemaphoreType.DMA((len(DP_KINDS), n_dp)),
            pltpu.SemaphoreType.DMA((len(DP_KINDS), n_dp)),
        ],
        compiler_params=pltpu.CompilerParams(
            collective_id=0, has_side_effects=True, vmem_limit_bytes=48 * 1024 * 1024
        ),
        name="attention_layer",
    )(
        qkvu, actions.reshape(1, rows), lengths, action_table,
        gain.reshape(1, width), w_out, cotangent,
    )
    output, d_qkvu, d_wout, d_table, d_gain = outs
    return output, d_qkvu, d_wout, d_table, d_gain.reshape(width)


def solution(mesh):
    both = P(("dp", "ctx"), None)
    return jax.shard_map(
        functools.partial(on_device, mesh.shape["ctx"], mesh.shape["dp"]),
        mesh=mesh,
        in_specs=(both, P(("dp", "ctx")), P("dp", None), P(), P(), P(), both),
        out_specs=(both, both, P("dp", None), P(), P()),
        check_vma=False,
    )
```

```python
import functools

import jax
import jax.numpy as jnp
from jax import lax
from jax.experimental import pallas as pl
from jax.experimental.pallas import tpu as pltpu
from jax.sharding import PartitionSpec as P

HD = 128
ACTIONS = 64
F32 = jnp.float32
BF16 = jnp.bfloat16
CTX_KINDS = ("kv", "q", "cot", "mix", "dout", "tab", "gain", "wfin", "tfin")
DP_KINDS = ("wdp", "tdp", "gdp")


def sigmoid(x):
    return 0.5 * jnp.tanh(0.5 * x) + 0.5


def silu_slope(x):
    sig = sigmoid(x)
    return sig * (1.0 + x * (1.0 - sig))


def dot_nn(a, b):
    return lax.dot_general(a, b, (((1,), (0,)), ((), ())), preferred_element_type=F32)


def dot_nt(a, b):
    return lax.dot_general(a, b, (((1,), (1,)), ((), ())), preferred_element_type=F32)


def dot_tn(a, b):
    return lax.dot_general(a, b, (((0,), (0,)), ((), ())), preferred_element_type=F32)


def layer_kernel(
    n_ctx, n_dp, f_parts,
    qkvu_in, act_in, len_in, table_in, gain_in, wout_in, cot_in,
    out_ref, dqkvu_ref, dwout_ref, dtable_ref, dgain_ref,
    kv_buf, q_buf, cot_buf, mix_buf, do_buf, tab_src, tab_buf, gain_buf,
    wdp_src, wdp_buf, tdp_src, tdp_buf, gdp_src, gdp_buf, wfin_buf, tfin_buf,
    p_q, w_k, p_k, acc, acc_k, acc_v, gm_ref, gate_ref, gslope_ref,
    qkvu_ref, act_ref, len_ref, table_ref, gain_ref, wout_ref, cot_ref,
    ctx_send, ctx_recv, relay_send, dp_send, dp_recv, load_sem,
):
    me = lax.axis_index("ctx")
    dpi = lax.axis_index("dp")
    rows = qkvu_ref.shape[0]
    width = wout_ref.shape[0]
    heads = width // HD
    scale = HD ** (-0.5)
    c_width = cot_buf.shape[2]
    dp_rows = dwout_ref.shape[0]
    p_rows = dp_rows // f_parts
    t_rows = tab_buf.shape[1]

    def ctx_copy(kind, src, dst, peer):
        k = CTX_KINDS.index(kind)
        return pltpu.make_async_remote_copy(
            src_ref=src, dst_ref=dst,
            send_sem=ctx_send.at[k, peer], recv_sem=ctx_recv.at[k, me],
            device_id={"ctx": peer}, device_id_type=pl.DeviceIdType.MESH,
        )

    def ctx_arrived(kind, buf, source):
        k = CTX_KINDS.index(kind)
        pltpu.make_async_remote_copy(
            src_ref=buf.at[source], dst_ref=buf.at[source],
            send_sem=ctx_send.at[k, source], recv_sem=ctx_recv.at[k, source],
            device_id={"ctx": source}, device_id_type=pl.DeviceIdType.MESH,
        ).wait_recv()

    def dp_copy(kind, src, dst, peer):
        k = DP_KINDS.index(kind)
        return pltpu.make_async_remote_copy(
            src_ref=src, dst_ref=dst,
            send_sem=dp_send.at[k, peer], recv_sem=dp_recv.at[k, dpi],
            device_id={"dp": peer}, device_id_type=pl.DeviceIdType.MESH,
        )

    def dp_arrived(kind, buf, source):
        k = DP_KINDS.index(kind)
        pltpu.make_async_remote_copy(
            src_ref=buf.at[source], dst_ref=buf.at[source],
            send_sem=dp_send.at[k, source], recv_sem=dp_recv.at[k, source],
            device_id={"dp": source}, device_id_type=pl.DeviceIdType.MESH,
        ).wait_recv()

    def ctx_peer(d):
        return lax.rem(me + d, n_ctx)

    def dp_peer(d):
        return lax.rem(dpi + d, n_dp)

    core = lax.rem(me, 2)
    chip = me // 2
    chips = n_ctx // 2
    sibling = me + 1 - 2 * core

    def relay_copy(kind, buf, slot):
        k = CTX_KINDS.index(kind)
        return pltpu.make_async_remote_copy(
            src_ref=buf.at[slot], dst_ref=buf.at[slot],
            send_sem=relay_send.at[k, slot], recv_sem=ctx_recv.at[k, slot],
            device_id={"ctx": sibling}, device_id_type=pl.DeviceIdType.MESH,
        )

    def relay(kind, buf, low, high):
        def step(c, carry):
            ctx_arrived(kind, buf, 2 * c + core)
            relay_copy(kind, buf, 2 * c + core).start()
            return carry

        lax.fori_loop(low, high, step, 0)

    def relay_wait(kind, buf, low, high):
        def step(c, carry):
            relay_copy(kind, buf, 2 * c + core).wait_send()
            return carry

        lax.fori_loop(low, high, step, 0)

    barrier = pltpu.get_barrier_semaphore()
    for d in range(1, n_ctx):
        pl.semaphore_signal(
            barrier, inc=1, device_id={"ctx": ctx_peer(d)}, device_id_type=pl.DeviceIdType.MESH
        )
    for d in range(1, n_dp):
        pl.semaphore_signal(
            barrier, inc=1, device_id={"dp": dp_peer(d)}, device_id_type=pl.DeviceIdType.MESH
        )

    qkvu_cols = [slice(b * width, (b + 1) * width) for b in range(4)]
    loads = [
        pltpu.make_async_copy(source, target, load_sem.at[n])
        for n, (source, target) in enumerate(
            [(qkvu_in.at[:, qkvu_cols[b]], qkvu_ref.at[:, qkvu_cols[b]]) for b in (3, 1, 2)]
            + [(cot_in, cot_ref), (wout_in, wout_ref), (len_in, len_ref)]
            + [(qkvu_in.at[:, qkvu_cols[0]], qkvu_ref.at[:, qkvu_cols[0]])]
            + [(table_in, table_ref), (act_in, act_ref), (gain_in, gain_ref)]
        )
    ]
    for load in loads:
        load.start()

    def activated(block):
        x = qkvu_ref[:, block * width : (block + 1) * width].astype(F32)
        return (x * sigmoid(x)).astype(BF16)

    loads[0].wait()
    kv_buf[me, :, :width] = activated(3)
    loads[1].wait()
    kv_buf[me, :, width:] = activated(1)
    loads[2].wait()
    q_buf[me] = activated(2)
    loads[3].wait()
    pl.semaphore_wait(barrier, n_ctx - 1 + n_dp - 1)

    def kv_copy(peer):
        return ctx_copy("kv", kv_buf.at[me], kv_buf.at[me], peer)

    def q_copy(peer):
        return ctx_copy("q", q_buf.at[me], q_buf.at[me], peer)

    def do_copy(peer):
        return ctx_copy("dout", do_buf.at[me], do_buf.at[me], peer)

    def cot_copy(peer):
        start = pl.multiple_of((peer // f_parts) * c_width, c_width)
        return ctx_copy("cot", cot_ref.at[:, pl.ds(start, c_width)], cot_buf.at[me], peer)

    def mix_copy(peer):
        return ctx_copy("mix", mix_buf.at[me], mix_buf.at[me], peer)

    def tab_copy(peer):
        return ctx_copy("tab", tab_src.at[peer], tab_buf.at[me], peer)

    def gain_copy(peer):
        return ctx_copy("gain", gain_buf.at[me], gain_buf.at[me], peer)

    def wfin_copy(peer):
        return ctx_copy("wfin", wfin_buf.at[me], wfin_buf.at[me], peer)

    def tfin_copy(peer):
        return ctx_copy("tfin", tfin_buf.at[me], tfin_buf.at[me], peer)

    part = lax.rem(me, f_parts)

    def wdp_copy(peer):
        start = pl.multiple_of(peer * dp_rows + part * p_rows, p_rows)
        return dp_copy("wdp", wdp_src.at[pl.ds(start, p_rows)], wdp_buf.at[dpi], peer)

    def tdp_copy(peer):
        return dp_copy("tdp", tdp_src, tdp_buf.at[dpi], peer)

    def gdp_copy(peer):
        return dp_copy("gdp", gdp_src, gdp_buf.at[dpi], peer)

    def for_higher(action):
        @pl.when(core == 0)
        def _():
            action(sibling)

        for d in range(1, chips):
            @pl.when(chip + d < chips)
            def _():
                action(me + 2 * d)

    def for_lower(action):
        @pl.when(core == 1)
        def _():
            action(sibling)

        for d in range(1, chips):
            @pl.when(chip >= d)
            def _():
                action(me - 2 * d)

    def for_partners(action):
        for d in range(1, chips):
            action(ctx_peer(2 * d))
        action(sibling)

    def for_others(action):
        for d in range(1, n_ctx):
            action(ctx_peer(d))

    def for_dp_others(action):
        for d in range(1, n_dp):
            action(dp_peer(d))

    for_higher(lambda p: kv_copy(p).start())
    for_lower(lambda p: q_copy(p).start())
    for_others(lambda p: cot_copy(p).start())
    own_start = pl.multiple_of((me // f_parts) * c_width, c_width)
    cot_buf[me] = cot_ref[:, pl.ds(own_start, c_width)]

    def history(pos):
        bound = jnp.int32(0)
        start = jnp.zeros_like(pos)
        length = jnp.zeros_like(pos)
        for s in range(len_ref.shape[1]):
            here = pos >= bound
            start = jnp.where(here, bound, start)
            length = jnp.where(here, len_ref[0, s], length)
            bound = bound + len_ref[0, s]
        return start, length

    sub = lax.broadcasted_iota(jnp.int32, (rows, rows), 0)
    lane = lax.broadcasted_iota(jnp.int32, (rows, rows), 1)

    def score_parts(s):
        sig = sigmoid(s)
        t = s * sig
        return t, sig + t * (1.0 - sig)

    def key_side_block(i):
        pos_q = i * rows + lane
        pos_k = me * rows + sub
        start, length = history(pos_q)
        allowed = (pos_k >= start) & (pos_k <= pos_q)
        factor = jnp.where(allowed, 1.0 / length.astype(F32), 0.0)
        for h in range(heads):
            cols = slice(h * HD, (h + 1) * HD)
            t, slope = score_parts(dot_nt(kv_buf[me, :, cols], q_buf[i, :, cols]) * scale)
            w_k[i, h] = (t * factor).astype(BF16)
            p_k[i, h] = slope * factor

    for load in loads[4:]:
        load.wait()

    onehot_t = (
        lax.broadcasted_iota(jnp.int32, (ACTIONS, rows), 0) == act_ref[...]
    ).astype(BF16)
    gate_pre = qkvu_ref[:, :width].astype(F32) + dot_tn(onehot_t, table_ref[...])
    gate_sig = sigmoid(gate_pre)
    gate_ref[...] = gate_pre * gate_sig
    gslope_ref[...] = gate_sig * (1.0 + gate_pre * (1.0 - gate_sig))
    gm_ref[...] = dot_nt(cot_ref[...], wout_ref[...])
    key_side_block(me)

    acc[...] = jnp.zeros_like(acc)

    def forward(j):
        pos_q = me * rows + sub
        pos_k = j * rows + lane
        start, length = history(pos_q)
        allowed = (pos_k >= start) & (pos_k <= pos_q)
        factor = jnp.where(allowed, 1.0 / length.astype(F32), 0.0)
        for h in range(heads):
            cols = slice(h * HD, (h + 1) * HD)
            vcols = slice(width + h * HD, width + (h + 1) * HD)
            t, slope = score_parts(dot_nt(q_buf[me, :, cols], kv_buf[j, :, cols]) * scale)
            p_q[j, h] = slope * factor
            acc[:, cols] += dot_nn((t * factor).astype(BF16), kv_buf[j, :, vcols])

    def forward_direct(c, carry):
        forward(2 * c + core)
        return carry

    def forward_relayed(c, carry):
        ctx_arrived("kv", kv_buf, 2 * c + 1 - core)
        forward(2 * c + 1 - core)
        return carry

    lax.fori_loop(chip, chip + 1, forward_direct, 0)

    @pl.when(core == 1)
    def _():
        ctx_arrived("kv", kv_buf, sibling)
        forward(sibling)

    relay("kv", kv_buf, 0, chip)
    lax.fori_loop(0, chip, forward_direct, 0)
    lax.fori_loop(0, chip, forward_relayed, 0)

    attended = acc[...]
    gain = gain_ref[...]
    gate = gate_ref[...]
    centre = attended - jnp.mean(attended, axis=1, keepdims=True)
    inv_std = lax.rsqrt(jnp.mean(centre * centre, axis=1, keepdims=True) + 1e-05)
    normed = centre * inv_std
    mixed = (normed * gain * gate).astype(BF16)
    mix_buf[me] = mixed
    for_partners(lambda p: mix_copy(p).start())
    grad_mixed = gm_ref[...]
    gated = grad_mixed * gate
    pushed = gated * gain
    grad_out = (
        pushed
        - jnp.mean(pushed, axis=1, keepdims=True)
        - normed * jnp.mean(pushed * normed, axis=1, keepdims=True)
    ) * inv_std
    do_buf[me] = grad_out.astype(BF16)
    for_lower(lambda p: do_copy(p).start())
    relay("mix", mix_buf, 0, chip)
    gain_buf[me] = jnp.sum(gated * normed, axis=0, keepdims=True)
    for_others(lambda p: gain_copy(p).start())
    grad_gate = grad_mixed * gain * normed * gslope_ref[...]
    dqkvu_ref[:, :width] = grad_gate.astype(BF16)
    high = grad_gate.astype(BF16)
    low = (grad_gate - high.astype(F32)).astype(BF16)
    table_term = dot_nn(onehot_t, high) + dot_nn(onehot_t, low)
    for s in range(n_ctx):
        tab_src[s] = table_term[s * t_rows : (s + 1) * t_rows]
    for_others(lambda p: tab_copy(p).start())
    tab_buf[me] = tab_src[me]
    relay("q", q_buf, chip + 1, chips)

    out_ref[...] = dot_nn(mixed, wout_ref[...]).astype(BF16)

    acc[...] = jnp.zeros_like(acc)

    def query_grad(step, carry):
        j = me - step
        for h in range(heads):
            cols = slice(h * HD, (h + 1) * HD)
            vcols = slice(width + h * HD, width + (h + 1) * HD)
            prod = dot_nt(do_buf[me, :, cols], kv_buf[j, :, vcols])
            acc[:, cols] += dot_nn((prod * p_q[j, h]).astype(BF16), kv_buf[j, :, cols])
        return carry

    lax.fori_loop(0, me + 1, query_grad, 0)
    q_pre = qkvu_ref[:, 2 * width : 3 * width].astype(F32)
    dqkvu_ref[:, 2 * width : 3 * width] = (acc[...] * scale * silu_slope(q_pre)).astype(BF16)

    @pl.when(core == 0)
    def _():
        ctx_arrived("q", q_buf, sibling)
        key_side_block(sibling)

    def key_side_direct(c, carry):
        key_side_block(2 * c + core)
        return carry

    def key_side_relayed(c, carry):
        ctx_arrived("q", q_buf, 2 * c + 1 - core)
        key_side_block(2 * c + 1 - core)
        return carry

    lax.fori_loop(chip + 1, chips, key_side_direct, 0)
    lax.fori_loop(chip + 1, chips, key_side_relayed, 0)
    relay("mix", mix_buf, chip + 1, chips)

    for_others(lambda p: ctx_arrived("gain", gain_buf, p))
    gain_sum = gain_buf[0]
    for s in range(1, n_ctx):
        gain_sum = gain_sum + gain_buf[s]
    gdp_src[...] = gain_sum
    for_dp_others(lambda p: gdp_copy(p).start())
    gdp_buf[dpi] = gain_sum
    for_others(lambda p: ctx_arrived("tab", tab_buf, p))
    tab_sum = tab_buf[0]
    for s in range(1, n_ctx):
        tab_sum = tab_sum + tab_buf[s]
    tdp_src[...] = tab_sum.astype(tdp_src.dtype)
    for_dp_others(lambda p: tdp_copy(p).start())
    tdp_buf[dpi] = tab_sum.astype(tdp_src.dtype)

    for_others(lambda p: ctx_arrived("cot", cot_buf, p))
    ctx_arrived("mix", mix_buf, sibling)
    for d in range(1, chips):
        ctx_arrived("mix", mix_buf, lax.rem(sibling + 2 * d, n_ctx))
    w_sum = dot_tn(
        mix_buf[...].reshape(n_ctx * rows, width), cot_buf[...].reshape(n_ctx * rows, c_width)
    )
    wdp_src[...] = w_sum.astype(wdp_src.dtype)
    for_dp_others(lambda p: wdp_copy(p).start())
    own_rows = pl.multiple_of(dpi * dp_rows + part * p_rows, p_rows)
    wdp_buf[dpi] = wdp_src[pl.ds(own_rows, p_rows)]

    acc_k[...] = jnp.zeros_like(acc_k)
    acc_v[...] = jnp.zeros_like(acc_v)

    def key_grad(i):
        for h in range(heads):
            cols = slice(h * HD, (h + 1) * HD)
            vcols = slice(width + h * HD, width + (h + 1) * HD)
            grads = do_buf[i, :, cols]
            prod = dot_nt(kv_buf[me, :, vcols], grads)
            acc_k[:, cols] += dot_nn((prod * p_k[i, h]).astype(BF16), q_buf[i, :, cols])
            acc_v[:, cols] += dot_nn(w_k[i, h], grads)

    def key_grad_direct(c, carry):
        key_grad(2 * c + core)
        return carry

    def key_grad_relayed(c, carry):
        ctx_arrived("dout", do_buf, 2 * c + 1 - core)
        key_grad(2 * c + 1 - core)
        return carry

    relay("dout", do_buf, chip + 1, chips)
    lax.fori_loop(chip, chips, key_grad_direct, 0)
    lax.fori_loop(chip + core, chips, key_grad_relayed, 0)
    v_pre = qkvu_ref[:, width : 2 * width].astype(F32)
    dqkvu_ref[:, width : 2 * width] = (acc_v[...] * silu_slope(v_pre)).astype(BF16)
    k_pre = qkvu_ref[:, 3 * width :].astype(F32)
    dqkvu_ref[:, 3 * width :] = (acc_k[...] * scale * silu_slope(k_pre)).astype(BF16)

    for_dp_others(lambda p: dp_arrived("tdp", tdp_buf, p))
    total = tdp_buf[0].astype(F32)
    for s in range(1, n_dp):
        total = total + tdp_buf[s].astype(F32)
    tfin_buf[me] = total
    for_others(lambda p: tfin_copy(p).start())
    for_dp_others(lambda p: dp_arrived("gdp", gdp_buf, p))
    total = gdp_buf[0]
    for s in range(1, n_dp):
        total = total + gdp_buf[s]
    dgain_ref[...] = total
    for_dp_others(lambda p: dp_arrived("wdp", wdp_buf, p))
    total = wdp_buf[0].astype(F32)
    for s in range(1, n_dp):
        total = total + wdp_buf[s].astype(F32)
    wfin_buf[me] = total.astype(wfin_buf.dtype)
    for_others(lambda p: wfin_copy(p).start())
    for_others(lambda p: ctx_arrived("tfin", tfin_buf, p))
    for s in range(n_ctx):
        dtable_ref[s * t_rows : (s + 1) * t_rows] = tfin_buf[s]
    for_others(lambda p: ctx_arrived("wfin", wfin_buf, p))
    for s in range(n_ctx):
        top, left = (s % f_parts) * p_rows, (s // f_parts) * c_width
        dwout_ref[top : top + p_rows, left : left + c_width] = wfin_buf[s].astype(F32)

    for_higher(lambda p: kv_copy(p).wait_send())
    for_lower(lambda p: q_copy(p).wait_send())
    for_lower(lambda p: do_copy(p).wait_send())
    for_partners(lambda p: mix_copy(p).wait_send())
    relay_wait("kv", kv_buf, 0, chip)
    relay_wait("q", q_buf, chip + 1, chips)
    relay_wait("dout", do_buf, chip + 1, chips)
    relay_wait("mix", mix_buf, 0, chip)
    relay_wait("mix", mix_buf, chip + 1, chips)
    for copy in (cot_copy, tab_copy, gain_copy, wfin_copy, tfin_copy):
        for_others(lambda p: copy(p).wait_send())
    for copy in (wdp_copy, tdp_copy, gdp_copy):
        for_dp_others(lambda p: copy(p).wait_send())


def store_kernel(*refs):
    sems = refs[10]
    stores = [pltpu.make_async_copy(refs[n], refs[5 + n], sems.at[n]) for n in range(5)]
    for store in stores:
        store.start()
    for store in stores:
        store.wait()


def on_device(n_ctx, n_dp, qkvu, actions, lengths, action_table, gain, w_out, cotangent):
    rows = qkvu.shape[0]
    width, model = w_out.shape
    heads = width // HD
    c_parts = min(n_ctx, model // 128)
    f_parts = n_ctx // c_parts
    c_width = model // c_parts
    dp_rows = width // n_dp
    p_rows = dp_rows // f_parts
    t_rows = ACTIONS // n_ctx
    w_kind = BF16 if p_rows % 16 == 0 else F32
    t_kind = BF16 if t_rows % 16 == 0 else F32
    vmem = pl.BlockSpec(memory_space=pltpu.VMEM)
    outs = pl.pallas_call(
        functools.partial(layer_kernel, n_ctx, n_dp, f_parts),
        out_shape=(
            jax.ShapeDtypeStruct((rows, model), BF16),
            jax.ShapeDtypeStruct((rows, 4 * width), BF16),
            jax.ShapeDtypeStruct((dp_rows, model), F32),
            jax.ShapeDtypeStruct((ACTIONS, width), F32),
            jax.ShapeDtypeStruct((1, width), F32),
        ),
        in_specs=[pl.BlockSpec(memory_space=pltpu.HBM)] * 7,
        out_specs=(vmem,) * 5,
        scratch_shapes=[
            pltpu.VMEM((n_ctx, rows, 2 * width), BF16),
            pltpu.VMEM((n_ctx, rows, width), BF16),
            pltpu.VMEM((n_ctx, rows, c_width), BF16),
            pltpu.VMEM((n_ctx, rows, width), BF16),
            pltpu.VMEM((n_ctx, rows, width), BF16),
            pltpu.VMEM((n_ctx, t_rows, width), F32),
            pltpu.VMEM((n_ctx, t_rows, width), F32),
            pltpu.VMEM((n_ctx, 1, width), F32),
            pltpu.VMEM((width, c_width), w_kind),
            pltpu.VMEM((n_dp, p_rows, c_width), w_kind),
            pltpu.VMEM((t_rows, width), t_kind),
            pltpu.VMEM((n_dp, t_rows, width), t_kind),
            pltpu.VMEM((1, width), F32),
            pltpu.VMEM((n_dp, 1, width), F32),
            pltpu.VMEM((n_ctx, p_rows, c_width), w_kind),
            pltpu.VMEM((n_ctx, t_rows, width), F32),
            pltpu.VMEM((n_ctx, heads, rows, rows), F32),
            pltpu.VMEM((n_ctx, heads, rows, rows), BF16),
            pltpu.VMEM((n_ctx, heads, rows, rows), F32),
            pltpu.VMEM((rows, width), F32),
            pltpu.VMEM((rows, width), F32),
            pltpu.VMEM((rows, width), F32),
            pltpu.VMEM((rows, width), F32),
            pltpu.VMEM((rows, width), F32),
            pltpu.VMEM((rows, width), F32),
            pltpu.VMEM((rows, 4 * width), BF16),
            pltpu.VMEM((1, rows), jnp.int32),
            pltpu.SMEM(lengths.shape, jnp.int32),
            pltpu.VMEM(action_table.shape, BF16),
            pltpu.VMEM((1, width), F32),
            pltpu.VMEM((width, model), BF16),
            pltpu.VMEM((rows, model), BF16),
            pltpu.SemaphoreType.DMA((len(CTX_KINDS), n_ctx)),
            pltpu.SemaphoreType.DMA((len(CTX_KINDS), n_ctx)),
            pltpu.SemaphoreType.DMA((len(CTX_KINDS), n_ctx)),
            pltpu.SemaphoreType.DMA((len(DP_KINDS), n_dp)),
            pltpu.SemaphoreType.DMA((len(DP_KINDS), n_dp)),
            pltpu.SemaphoreType.DMA((10,)),
        ],
        compiler_params=pltpu.CompilerParams(
            collective_id=0, has_side_effects=True, vmem_limit_bytes=48 * 1024 * 1024
        ),
        name="attention_layer",
    )(
        qkvu, actions.reshape(1, rows), lengths, action_table,
        gain.reshape(1, width), w_out, cotangent,
    )
    output, d_qkvu, d_wout, d_table, d_gain = pl.pallas_call(
        store_kernel,
        out_shape=[jax.ShapeDtypeStruct(o.shape, o.dtype) for o in outs],
        in_specs=[vmem] * 5,
        out_specs=[pl.BlockSpec(memory_space=pl.ANY)] * 5,
        scratch_shapes=[pltpu.SemaphoreType.DMA((5,))],
        name="store_results",
    )(*outs)
    return output, d_qkvu, d_wout, d_table, d_gain.reshape(width)


def solution(mesh):
    both = P(("dp", "ctx"), None)
    return jax.shard_map(
        functools.partial(on_device, mesh.shape["ctx"], mesh.shape["dp"]),
        mesh=mesh,
        in_specs=(both, P(("dp", "ctx")), P("dp", None), P(), P(), P(), both),
        out_specs=(both, both, P("dp", None), P(), P()),
        check_vma=False,
    )
```

```python
import functools

import jax
import jax.numpy as jnp
from jax import lax
from jax.experimental import pallas as pl
from jax.experimental.pallas import tpu as pltpu
from jax.sharding import PartitionSpec as P

HD = 128
ACTIONS = 64
F32 = jnp.float32
BF16 = jnp.bfloat16
CTX_KINDS = ("kv", "q", "cot", "mix", "dout", "tab", "gain", "wfin", "tfin")
DP_KINDS = ("wdp", "tdp", "gdp")


def sigmoid(x):
    return 0.5 * jnp.tanh(0.5 * x) + 0.5


def silu_slope(x):
    sig = sigmoid(x)
    return sig * (1.0 + x * (1.0 - sig))


def dot_nn(a, b):
    return lax.dot_general(a, b, (((1,), (0,)), ((), ())), preferred_element_type=F32)


def dot_nt(a, b):
    return lax.dot_general(a, b, (((1,), (1,)), ((), ())), preferred_element_type=F32)


def dot_tn(a, b):
    return lax.dot_general(a, b, (((0,), (0,)), ((), ())), preferred_element_type=F32)


def layer_kernel(
    n_ctx, n_dp, f_parts,
    qkvu_in, act_in, len_in, table_in, gain_in, wout_in, cot_in,
    out_ref, dqkvu_ref, dwout_ref, dtable_ref, dgain_ref,
    kv_buf, q_buf, cot_buf, mix_buf, do_buf, tab_src, tab_buf, gain_buf,
    wdp_src, wdp_buf, tdp_src, tdp_buf, gdp_src, gdp_buf, wfin_buf, tfin_buf,
    p_q, w_k, p_k, acc, acc_k, acc_v, gm_ref, gate_ref, gslope_ref,
    qkvu_ref, act_ref, len_ref, table_ref, gain_ref, wout_ref, cot_ref,
    ctx_send, ctx_recv, relay_send, dp_send, dp_recv, load_sem,
):
    me = lax.axis_index("ctx")
    dpi = lax.axis_index("dp")
    rows = qkvu_ref.shape[0]
    width = wout_ref.shape[0]
    heads = width // HD
    scale = HD ** (-0.5)
    c_width = cot_buf.shape[2]
    dp_rows = dwout_ref.shape[0]
    p_rows = dp_rows // f_parts
    t_rows = tab_buf.shape[1]

    def ctx_copy(kind, src, dst, peer):
        k = CTX_KINDS.index(kind)
        return pltpu.make_async_remote_copy(
            src_ref=src, dst_ref=dst,
            send_sem=ctx_send.at[k, peer], recv_sem=ctx_recv.at[k, me],
            device_id={"ctx": peer}, device_id_type=pl.DeviceIdType.MESH,
        )

    def ctx_arrived(kind, buf, source):
        k = CTX_KINDS.index(kind)
        pltpu.make_async_remote_copy(
            src_ref=buf.at[source], dst_ref=buf.at[source],
            send_sem=ctx_send.at[k, source], recv_sem=ctx_recv.at[k, source],
            device_id={"ctx": source}, device_id_type=pl.DeviceIdType.MESH,
        ).wait_recv()

    def dp_copy(kind, src, dst, peer):
        k = DP_KINDS.index(kind)
        return pltpu.make_async_remote_copy(
            src_ref=src, dst_ref=dst,
            send_sem=dp_send.at[k, peer], recv_sem=dp_recv.at[k, dpi],
            device_id={"dp": peer}, device_id_type=pl.DeviceIdType.MESH,
        )

    def dp_arrived(kind, buf, source):
        k = DP_KINDS.index(kind)
        pltpu.make_async_remote_copy(
            src_ref=buf.at[source], dst_ref=buf.at[source],
            send_sem=dp_send.at[k, source], recv_sem=dp_recv.at[k, source],
            device_id={"dp": source}, device_id_type=pl.DeviceIdType.MESH,
        ).wait_recv()

    def ctx_peer(d):
        return lax.rem(me + d, n_ctx)

    def dp_peer(d):
        return lax.rem(dpi + d, n_dp)

    core = lax.rem(me, 2)
    chip = me // 2
    chips = n_ctx // 2
    sibling = me + 1 - 2 * core

    def relay_copy(kind, buf, slot):
        k = CTX_KINDS.index(kind)
        return pltpu.make_async_remote_copy(
            src_ref=buf.at[slot], dst_ref=buf.at[slot],
            send_sem=relay_send.at[k, slot], recv_sem=ctx_recv.at[k, slot],
            device_id={"ctx": sibling}, device_id_type=pl.DeviceIdType.MESH,
        )

    def relay(kind, buf, low, high):
        def step(c, carry):
            ctx_arrived(kind, buf, 2 * c + core)
            relay_copy(kind, buf, 2 * c + core).start()
            return carry

        lax.fori_loop(low, high, step, 0)

    def relay_wait(kind, buf, low, high):
        def step(c, carry):
            relay_copy(kind, buf, 2 * c + core).wait_send()
            return carry

        lax.fori_loop(low, high, step, 0)

    barrier = pltpu.get_barrier_semaphore()
    for d in range(1, n_ctx):
        pl.semaphore_signal(
            barrier, inc=1, device_id={"ctx": ctx_peer(d)}, device_id_type=pl.DeviceIdType.MESH
        )
    for d in range(1, n_dp):
        pl.semaphore_signal(
            barrier, inc=1, device_id={"dp": dp_peer(d)}, device_id_type=pl.DeviceIdType.MESH
        )

    qkvu_cols = [slice(b * width, (b + 1) * width) for b in range(4)]
    loads = [
        pltpu.make_async_copy(source, target, load_sem.at[n])
        for n, (source, target) in enumerate(
            [(qkvu_in.at[:, qkvu_cols[b]], qkvu_ref.at[:, qkvu_cols[b]]) for b in (3, 1, 2)]
            + [(cot_in, cot_ref), (wout_in, wout_ref), (len_in, len_ref)]
            + [(qkvu_in.at[:, qkvu_cols[0]], qkvu_ref.at[:, qkvu_cols[0]])]
            + [(table_in, table_ref), (act_in, act_ref), (gain_in, gain_ref)]
        )
    ]
    for load in loads:
        load.start()

    def activated(block):
        x = qkvu_ref[:, block * width : (block + 1) * width].astype(F32)
        return (x * sigmoid(x)).astype(BF16)

    loads[0].wait()
    kv_buf[me, :, :width] = activated(3)
    loads[1].wait()
    kv_buf[me, :, width:] = activated(1)
    loads[2].wait()
    q_buf[me] = activated(2)
    loads[3].wait()
    pl.semaphore_wait(barrier, n_ctx - 1 + n_dp - 1)

    def kv_copy(peer):
        return ctx_copy("kv", kv_buf.at[me], kv_buf.at[me], peer)

    def q_copy(peer):
        return ctx_copy("q", q_buf.at[me], q_buf.at[me], peer)

    def do_copy(peer):
        return ctx_copy("dout", do_buf.at[me], do_buf.at[me], peer)

    def cot_copy(peer):
        start = pl.multiple_of((peer // f_parts) * c_width, c_width)
        return ctx_copy("cot", cot_ref.at[:, pl.ds(start, c_width)], cot_buf.at[me], peer)

    def mix_copy(peer):
        return ctx_copy("mix", mix_buf.at[me], mix_buf.at[me], peer)

    def tab_copy(peer):
        return ctx_copy("tab", tab_src.at[peer], tab_buf.at[me], peer)

    def gain_copy(peer):
        return ctx_copy("gain", gain_buf.at[me], gain_buf.at[me], peer)

    def wfin_copy(peer):
        return ctx_copy("wfin", wfin_buf.at[me], wfin_buf.at[me], peer)

    def tfin_copy(peer):
        return ctx_copy("tfin", tfin_buf.at[me], tfin_buf.at[me], peer)

    part = lax.rem(me, f_parts)

    def wdp_copy(peer):
        start = pl.multiple_of(peer * dp_rows + part * p_rows, p_rows)
        return dp_copy("wdp", wdp_src.at[pl.ds(start, p_rows)], wdp_buf.at[dpi], peer)

    def tdp_copy(peer):
        return dp_copy("tdp", tdp_src, tdp_buf.at[dpi], peer)

    def gdp_copy(peer):
        return dp_copy("gdp", gdp_src, gdp_buf.at[dpi], peer)

    def for_higher(action):
        @pl.when(core == 0)
        def _():
            action(sibling)

        for d in range(1, chips):
            @pl.when(chip + d < chips)
            def _():
                action(me + 2 * d)

    def for_lower(action):
        @pl.when(core == 1)
        def _():
            action(sibling)

        for d in range(1, chips):
            @pl.when(chip >= d)
            def _():
                action(me - 2 * d)

    def for_partners(action):
        for d in range(1, chips):
            action(ctx_peer(2 * d))
        action(sibling)

    def for_others(action):
        for d in range(1, n_ctx):
            action(ctx_peer(d))

    def for_dp_others(action):
        for d in range(1, n_dp):
            action(dp_peer(d))

    for_higher(lambda p: kv_copy(p).start())
    for_lower(lambda p: q_copy(p).start())
    for_others(lambda p: cot_copy(p).start())
    own_start = pl.multiple_of((me // f_parts) * c_width, c_width)
    cot_buf[me] = cot_ref[:, pl.ds(own_start, c_width)]

    def history(pos):
        bound = jnp.int32(0)
        start = jnp.zeros_like(pos)
        length = jnp.zeros_like(pos)
        for s in range(len_ref.shape[1]):
            here = pos >= bound
            start = jnp.where(here, bound, start)
            length = jnp.where(here, len_ref[0, s], length)
            bound = bound + len_ref[0, s]
        return start, length

    sub = lax.broadcasted_iota(jnp.int32, (rows, rows), 0)
    lane = lax.broadcasted_iota(jnp.int32, (rows, rows), 1)

    def score_parts(s):
        sig = sigmoid(s)
        t = s * sig
        return t, sig + t * (1.0 - sig)

    def key_side_block(i):
        pos_q = i * rows + lane
        pos_k = me * rows + sub
        start, length = history(pos_q)
        allowed = (pos_k >= start) & (pos_k <= pos_q)
        factor = jnp.where(allowed, 1.0 / length.astype(F32), 0.0)
        for h in range(heads):
            cols = slice(h * HD, (h + 1) * HD)
            t, slope = score_parts(dot_nt(kv_buf[me, :, cols], q_buf[i, :, cols]) * scale)
            w_k[i, h] = (t * factor).astype(BF16)
            p_k[i, h] = slope * factor

    for load in loads[4:]:
        load.wait()

    onehot_t = (
        lax.broadcasted_iota(jnp.int32, (ACTIONS, rows), 0) == act_ref[...]
    ).astype(BF16)
    gate_pre = qkvu_ref[:, :width].astype(F32) + dot_tn(onehot_t, table_ref[...])
    gate_sig = sigmoid(gate_pre)
    gate_ref[...] = gate_pre * gate_sig
    gslope_ref[...] = gate_sig * (1.0 + gate_pre * (1.0 - gate_sig))
    gm_ref[...] = dot_nt(cot_ref[...], wout_ref[...])
    key_side_block(me)

    acc[...] = jnp.zeros_like(acc)

    def forward(j):
        pos_q = me * rows + sub
        pos_k = j * rows + lane
        start, length = history(pos_q)
        allowed = (pos_k >= start) & (pos_k <= pos_q)
        factor = jnp.where(allowed, 1.0 / length.astype(F32), 0.0)
        for h in range(heads):
            cols = slice(h * HD, (h + 1) * HD)
            vcols = slice(width + h * HD, width + (h + 1) * HD)
            t, slope = score_parts(dot_nt(q_buf[me, :, cols], kv_buf[j, :, cols]) * scale)
            p_q[j, h] = slope * factor
            acc[:, cols] += dot_nn((t * factor).astype(BF16), kv_buf[j, :, vcols])

    def forward_direct(c, carry):
        forward(2 * c + core)
        return carry

    def forward_relayed(c, carry):
        ctx_arrived("kv", kv_buf, 2 * c + 1 - core)
        forward(2 * c + 1 - core)
        return carry

    lax.fori_loop(chip, chip + 1, forward_direct, 0)

    @pl.when(core == 1)
    def _():
        ctx_arrived("kv", kv_buf, sibling)
        forward(sibling)

    relay("kv", kv_buf, 0, chip)
    lax.fori_loop(0, chip, forward_direct, 0)
    lax.fori_loop(0, chip, forward_relayed, 0)

    attended = acc[...]
    gain = gain_ref[...]
    gate = gate_ref[...]
    centre = attended - jnp.mean(attended, axis=1, keepdims=True)
    inv_std = lax.rsqrt(jnp.mean(centre * centre, axis=1, keepdims=True) + 1e-05)
    normed = centre * inv_std
    mixed = (normed * gain * gate).astype(BF16)
    mix_buf[me] = mixed
    for_partners(lambda p: mix_copy(p).start())
    grad_mixed = gm_ref[...]
    gated = grad_mixed * gate
    pushed = gated * gain
    grad_out = (
        pushed
        - jnp.mean(pushed, axis=1, keepdims=True)
        - normed * jnp.mean(pushed * normed, axis=1, keepdims=True)
    ) * inv_std
    do_buf[me] = grad_out.astype(BF16)
    for_lower(lambda p: do_copy(p).start())
    relay("mix", mix_buf, 0, chip)
    gain_buf[me] = jnp.sum(gated * normed, axis=0, keepdims=True)
    for_others(lambda p: gain_copy(p).start())
    grad_gate = grad_mixed * gain * normed * gslope_ref[...]
    dqkvu_ref[:, :width] = grad_gate.astype(BF16)
    high = grad_gate.astype(BF16)
    low = (grad_gate - high.astype(F32)).astype(BF16)
    table_term = dot_nn(onehot_t, high) + dot_nn(onehot_t, low)
    for s in range(n_ctx):
        tab_src[s] = table_term[s * t_rows : (s + 1) * t_rows]
    for_others(lambda p: tab_copy(p).start())
    tab_buf[me] = tab_src[me]
    relay("q", q_buf, chip + 1, chips)

    out_ref[...] = dot_nn(mixed, wout_ref[...]).astype(BF16)

    acc[...] = jnp.zeros_like(acc)

    def query_grad(step, carry):
        j = me - step
        for h in range(heads):
            cols = slice(h * HD, (h + 1) * HD)
            vcols = slice(width + h * HD, width + (h + 1) * HD)
            prod = dot_nt(do_buf[me, :, cols], kv_buf[j, :, vcols])
            acc[:, cols] += dot_nn((prod * p_q[j, h]).astype(BF16), kv_buf[j, :, cols])
        return carry

    lax.fori_loop(0, me + 1, query_grad, 0)
    q_pre = qkvu_ref[:, 2 * width : 3 * width].astype(F32)
    dqkvu_ref[:, 2 * width : 3 * width] = (acc[...] * scale * silu_slope(q_pre)).astype(BF16)

    @pl.when(core == 0)
    def _():
        ctx_arrived("q", q_buf, sibling)
        key_side_block(sibling)

    def key_side_direct(c, carry):
        key_side_block(2 * c + core)
        return carry

    def key_side_relayed(c, carry):
        ctx_arrived("q", q_buf, 2 * c + 1 - core)
        key_side_block(2 * c + 1 - core)
        return carry

    lax.fori_loop(chip + 1, chips, key_side_direct, 0)
    lax.fori_loop(chip + 1, chips, key_side_relayed, 0)
    relay("mix", mix_buf, chip + 1, chips)

    for_others(lambda p: ctx_arrived("gain", gain_buf, p))
    gain_sum = gain_buf[0]
    for s in range(1, n_ctx):
        gain_sum = gain_sum + gain_buf[s]
    gdp_src[...] = gain_sum
    for_dp_others(lambda p: gdp_copy(p).start())
    gdp_buf[dpi] = gain_sum
    for_others(lambda p: ctx_arrived("tab", tab_buf, p))
    tab_sum = tab_buf[0]
    for s in range(1, n_ctx):
        tab_sum = tab_sum + tab_buf[s]
    tdp_src[...] = tab_sum.astype(tdp_src.dtype)
    for_dp_others(lambda p: tdp_copy(p).start())
    tdp_buf[dpi] = tab_sum.astype(tdp_src.dtype)

    for_others(lambda p: ctx_arrived("cot", cot_buf, p))
    ctx_arrived("mix", mix_buf, sibling)
    for d in range(1, chips):
        ctx_arrived("mix", mix_buf, lax.rem(sibling + 2 * d, n_ctx))
    w_sum = dot_tn(
        mix_buf[...].reshape(n_ctx * rows, width), cot_buf[...].reshape(n_ctx * rows, c_width)
    )
    wdp_src[...] = w_sum.astype(wdp_src.dtype)
    for_dp_others(lambda p: wdp_copy(p).start())
    own_rows = pl.multiple_of(dpi * dp_rows + part * p_rows, p_rows)
    wdp_buf[dpi] = wdp_src[pl.ds(own_rows, p_rows)]

    acc_k[...] = jnp.zeros_like(acc_k)
    acc_v[...] = jnp.zeros_like(acc_v)

    def key_grad(i):
        for h in range(heads):
            cols = slice(h * HD, (h + 1) * HD)
            vcols = slice(width + h * HD, width + (h + 1) * HD)
            grads = do_buf[i, :, cols]
            prod = dot_nt(kv_buf[me, :, vcols], grads)
            acc_k[:, cols] += dot_nn((prod * p_k[i, h]).astype(BF16), q_buf[i, :, cols])
            acc_v[:, cols] += dot_nn(w_k[i, h], grads)

    def key_grad_direct(c, carry):
        key_grad(2 * c + core)
        return carry

    def key_grad_relayed(c, carry):
        ctx_arrived("dout", do_buf, 2 * c + 1 - core)
        key_grad(2 * c + 1 - core)
        return carry

    relay("dout", do_buf, chip + 1, chips)
    lax.fori_loop(chip, chips, key_grad_direct, 0)
    lax.fori_loop(chip + core, chips, key_grad_relayed, 0)
    v_pre = qkvu_ref[:, width : 2 * width].astype(F32)
    dqkvu_ref[:, width : 2 * width] = (acc_v[...] * silu_slope(v_pre)).astype(BF16)
    k_pre = qkvu_ref[:, 3 * width :].astype(F32)
    dqkvu_ref[:, 3 * width :] = (acc_k[...] * scale * silu_slope(k_pre)).astype(BF16)

    for_dp_others(lambda p: dp_arrived("tdp", tdp_buf, p))
    total = tdp_buf[0].astype(F32)
    for s in range(1, n_dp):
        total = total + tdp_buf[s].astype(F32)
    tfin_buf[me] = total
    for_others(lambda p: tfin_copy(p).start())
    for_dp_others(lambda p: dp_arrived("gdp", gdp_buf, p))
    total = gdp_buf[0]
    for s in range(1, n_dp):
        total = total + gdp_buf[s]
    dgain_ref[...] = total
    for_dp_others(lambda p: dp_arrived("wdp", wdp_buf, p))
    total = wdp_buf[0].astype(F32)
    for s in range(1, n_dp):
        total = total + wdp_buf[s].astype(F32)
    wfin_buf[me] = total.astype(wfin_buf.dtype)
    for_others(lambda p: wfin_copy(p).start())
    for_others(lambda p: ctx_arrived("tfin", tfin_buf, p))
    for s in range(n_ctx):
        dtable_ref[s * t_rows : (s + 1) * t_rows] = tfin_buf[s]
    for_others(lambda p: ctx_arrived("wfin", wfin_buf, p))
    for s in range(n_ctx):
        top, left = (s % f_parts) * p_rows, (s // f_parts) * c_width
        dwout_ref[top : top + p_rows, left : left + c_width] = wfin_buf[s].astype(F32)

    for_higher(lambda p: kv_copy(p).wait_send())
    for_lower(lambda p: q_copy(p).wait_send())
    for_lower(lambda p: do_copy(p).wait_send())
    for_partners(lambda p: mix_copy(p).wait_send())
    relay_wait("kv", kv_buf, 0, chip)
    relay_wait("q", q_buf, chip + 1, chips)
    relay_wait("dout", do_buf, chip + 1, chips)
    relay_wait("mix", mix_buf, 0, chip)
    relay_wait("mix", mix_buf, chip + 1, chips)
    for copy in (cot_copy, tab_copy, gain_copy, wfin_copy, tfin_copy):
        for_others(lambda p: copy(p).wait_send())
    for copy in (wdp_copy, tdp_copy, gdp_copy):
        for_dp_others(lambda p: copy(p).wait_send())


def store_kernel(*refs):
    sems = refs[10]
    stores = [pltpu.make_async_copy(refs[n], refs[5 + n], sems.at[n]) for n in range(5)]
    for store in stores:
        store.start()
    for store in stores:
        store.wait()


def on_device(n_ctx, n_dp, qkvu, actions, lengths, action_table, gain, w_out, cotangent):
    rows = qkvu.shape[0]
    width, model = w_out.shape
    heads = width // HD
    c_parts = min(n_ctx, model // 128)
    f_parts = n_ctx // c_parts
    c_width = model // c_parts
    dp_rows = width // n_dp
    p_rows = dp_rows // f_parts
    t_rows = ACTIONS // n_ctx
    w_kind = BF16 if p_rows % 16 == 0 else F32
    t_kind = BF16 if t_rows % 16 == 0 else F32
    vmem = pl.BlockSpec(memory_space=pltpu.VMEM)
    outs = pl.pallas_call(
        functools.partial(layer_kernel, n_ctx, n_dp, f_parts),
        out_shape=(
            jax.ShapeDtypeStruct((rows, model), BF16),
            jax.ShapeDtypeStruct((rows, 4 * width), BF16),
            jax.ShapeDtypeStruct((dp_rows, model), F32),
            jax.ShapeDtypeStruct((ACTIONS, width), F32),
            jax.ShapeDtypeStruct((1, width), F32),
        ),
        in_specs=[pl.BlockSpec(memory_space=pltpu.HBM)] * 7,
        out_specs=(vmem,) * 5,
        scratch_shapes=[
            pltpu.VMEM((n_ctx, rows, 2 * width), BF16),
            pltpu.VMEM((n_ctx, rows, width), BF16),
            pltpu.VMEM((n_ctx, rows, c_width), BF16),
            pltpu.VMEM((n_ctx, rows, width), BF16),
            pltpu.VMEM((n_ctx, rows, width), BF16),
            pltpu.VMEM((n_ctx, t_rows, width), F32),
            pltpu.VMEM((n_ctx, t_rows, width), F32),
            pltpu.VMEM((n_ctx, 1, width), F32),
            pltpu.VMEM((width, c_width), w_kind),
            pltpu.VMEM((n_dp, p_rows, c_width), w_kind),
            pltpu.VMEM((t_rows, width), t_kind),
            pltpu.VMEM((n_dp, t_rows, width), t_kind),
            pltpu.VMEM((1, width), F32),
            pltpu.VMEM((n_dp, 1, width), F32),
            pltpu.VMEM((n_ctx, p_rows, c_width), w_kind),
            pltpu.VMEM((n_ctx, t_rows, width), F32),
            pltpu.VMEM((n_ctx, heads, rows, rows), F32),
            pltpu.VMEM((n_ctx, heads, rows, rows), BF16),
            pltpu.VMEM((n_ctx, heads, rows, rows), F32),
            pltpu.VMEM((rows, width), F32),
            pltpu.VMEM((rows, width), F32),
            pltpu.VMEM((rows, width), F32),
            pltpu.VMEM((rows, width), F32),
            pltpu.VMEM((rows, width), F32),
            pltpu.VMEM((rows, width), F32),
            pltpu.VMEM((rows, 4 * width), BF16),
            pltpu.VMEM((1, rows), jnp.int32),
            pltpu.SMEM(lengths.shape, jnp.int32),
            pltpu.VMEM(action_table.shape, BF16),
            pltpu.VMEM((1, width), F32),
            pltpu.VMEM((width, model), BF16),
            pltpu.VMEM((rows, model), BF16),
            pltpu.SemaphoreType.DMA((len(CTX_KINDS), n_ctx)),
            pltpu.SemaphoreType.DMA((len(CTX_KINDS), n_ctx)),
            pltpu.SemaphoreType.DMA((len(CTX_KINDS), n_ctx)),
            pltpu.SemaphoreType.DMA((len(DP_KINDS), n_dp)),
            pltpu.SemaphoreType.DMA((len(DP_KINDS), n_dp)),
            pltpu.SemaphoreType.DMA((10,)),
        ],
        compiler_params=pltpu.CompilerParams(
            collective_id=0, has_side_effects=True, vmem_limit_bytes=64 * 1024 * 1024
        ),
        name="attention_layer",
    )(
        qkvu, actions.reshape(1, rows), lengths, action_table,
        gain.reshape(1, width), w_out, cotangent,
    )
    output, d_qkvu, d_wout, d_table, d_gain = pl.pallas_call(
        store_kernel,
        out_shape=[jax.ShapeDtypeStruct(o.shape, o.dtype) for o in outs],
        in_specs=[pl.BlockSpec(memory_space=pl.ANY)] * 5,
        out_specs=[pl.BlockSpec(memory_space=pl.ANY)] * 5,
        scratch_shapes=[pltpu.SemaphoreType.DMA((5,))],
        compiler_params=pltpu.CompilerParams(vmem_limit_bytes=64 * 1024 * 1024),
        name="store_results",
    )(*outs)
    return output, d_qkvu, d_wout, d_table, d_gain.reshape(width)


def solution(mesh):
    both = P(("dp", "ctx"), None)
    return jax.shard_map(
        functools.partial(on_device, mesh.shape["ctx"], mesh.shape["dp"]),
        mesh=mesh,
        in_specs=(both, P(("dp", "ctx")), P("dp", None), P(), P(), P(), both),
        out_specs=(both, both, P("dp", None), P(), P()),
        check_vma=False,
    )
```

```python
import functools

import jax
import jax.numpy as jnp
from jax import lax
from jax.experimental import pallas as pl
from jax.experimental.pallas import tpu as pltpu
from jax.sharding import PartitionSpec as P

HD = 128
ACTIONS = 64
F32 = jnp.float32
BF16 = jnp.bfloat16
CTX_KINDS = ("kv", "q", "cot", "mix", "dout", "tab", "gain", "wfin", "tfin")
DP_KINDS = ("wdp", "tdp", "gdp")


def sigmoid(x):
    return 0.5 * jnp.tanh(0.5 * x) + 0.5


def silu_slope(x):
    sig = sigmoid(x)
    return sig * (1.0 + x * (1.0 - sig))


def dot_nn(a, b):
    return lax.dot_general(a, b, (((1,), (0,)), ((), ())), preferred_element_type=F32)


def dot_nt(a, b):
    return lax.dot_general(a, b, (((1,), (1,)), ((), ())), preferred_element_type=F32)


def dot_tn(a, b):
    return lax.dot_general(a, b, (((0,), (0,)), ((), ())), preferred_element_type=F32)


def layer_kernel(
    n_ctx, n_dp, f_parts,
    qkvu_in, act_in, len_in, table_in, gain_in, wout_in, cot_in,
    out_ref, dqkvu_ref, dwout_ref, dtable_ref, dgain_ref,
    kv_buf, q_buf, cot_buf, mix_buf, do_buf, tab_src, tab_buf, gain_buf,
    wdp_src, wdp_buf, tdp_src, tdp_buf, gdp_src, gdp_buf, wfin_buf, tfin_buf,
    p_q, w_k, p_k, acc, acc_k, acc_v, gm_ref, gate_ref, gslope_ref,
    qkvu_ref, act_ref, len_ref, table_ref, gain_ref, wout_ref, cot_ref,
    ctx_send, ctx_recv, relay_send, dp_send, dp_recv, load_sem,
):
    me = lax.axis_index("ctx")
    dpi = lax.axis_index("dp")
    rows = qkvu_ref.shape[0]
    width = wout_ref.shape[0]
    heads = width // HD
    scale = HD ** (-0.5)
    c_width = cot_buf.shape[2]
    dp_rows = dwout_ref.shape[0]
    p_rows = dp_rows // f_parts
    t_rows = tab_buf.shape[1]

    def ctx_copy(kind, src, dst, peer):
        k = CTX_KINDS.index(kind)
        return pltpu.make_async_remote_copy(
            src_ref=src, dst_ref=dst,
            send_sem=ctx_send.at[k, peer], recv_sem=ctx_recv.at[k, me],
            device_id={"ctx": peer}, device_id_type=pl.DeviceIdType.MESH,
        )

    def ctx_arrived(kind, buf, source):
        k = CTX_KINDS.index(kind)
        pltpu.make_async_remote_copy(
            src_ref=buf.at[source], dst_ref=buf.at[source],
            send_sem=ctx_send.at[k, source], recv_sem=ctx_recv.at[k, source],
            device_id={"ctx": source}, device_id_type=pl.DeviceIdType.MESH,
        ).wait_recv()

    def dp_copy(kind, src, dst, peer):
        k = DP_KINDS.index(kind)
        return pltpu.make_async_remote_copy(
            src_ref=src, dst_ref=dst,
            send_sem=dp_send.at[k, peer], recv_sem=dp_recv.at[k, dpi],
            device_id={"dp": peer}, device_id_type=pl.DeviceIdType.MESH,
        )

    def dp_arrived(kind, buf, source):
        k = DP_KINDS.index(kind)
        pltpu.make_async_remote_copy(
            src_ref=buf.at[source], dst_ref=buf.at[source],
            send_sem=dp_send.at[k, source], recv_sem=dp_recv.at[k, source],
            device_id={"dp": source}, device_id_type=pl.DeviceIdType.MESH,
        ).wait_recv()

    def ctx_peer(d):
        return lax.rem(me + d, n_ctx)

    def dp_peer(d):
        return lax.rem(dpi + d, n_dp)

    core = lax.rem(me, 2)
    chip = me // 2
    chips = n_ctx // 2
    sibling = me + 1 - 2 * core

    def relay_copy(kind, buf, slot):
        k = CTX_KINDS.index(kind)
        return pltpu.make_async_remote_copy(
            src_ref=buf.at[slot], dst_ref=buf.at[slot],
            send_sem=relay_send.at[k, slot], recv_sem=ctx_recv.at[k, slot],
            device_id={"ctx": sibling}, device_id_type=pl.DeviceIdType.MESH,
        )

    def relay(kind, buf, low, high):
        def step(c, carry):
            ctx_arrived(kind, buf, 2 * c + core)
            relay_copy(kind, buf, 2 * c + core).start()
            return carry

        lax.fori_loop(low, high, step, 0)

    def relay_wait(kind, buf, low, high):
        def step(c, carry):
            relay_copy(kind, buf, 2 * c + core).wait_send()
            return carry

        lax.fori_loop(low, high, step, 0)

    barrier = pltpu.get_barrier_semaphore()
    for d in range(1, n_ctx):
        pl.semaphore_signal(
            barrier, inc=1, device_id={"ctx": ctx_peer(d)}, device_id_type=pl.DeviceIdType.MESH
        )
    for d in range(1, n_dp):
        pl.semaphore_signal(
            barrier, inc=1, device_id={"dp": dp_peer(d)}, device_id_type=pl.DeviceIdType.MESH
        )

    qkvu_cols = [slice(b * width, (b + 1) * width) for b in range(4)]
    loads = [
        pltpu.make_async_copy(source, target, load_sem.at[n])
        for n, (source, target) in enumerate(
            [(qkvu_in.at[:, qkvu_cols[b]], qkvu_ref.at[:, qkvu_cols[b]]) for b in (3, 1, 2)]
            + [(cot_in, cot_ref), (wout_in, wout_ref), (len_in, len_ref)]
            + [(qkvu_in.at[:, qkvu_cols[0]], qkvu_ref.at[:, qkvu_cols[0]])]
            + [(table_in, table_ref), (act_in, act_ref), (gain_in, gain_ref)]
        )
    ]
    for load in loads:
        load.start()

    def activated(block):
        x = qkvu_ref[:, block * width : (block + 1) * width].astype(F32)
        return (x * sigmoid(x)).astype(BF16)

    loads[0].wait()
    kv_buf[me, :, :width] = activated(3)
    loads[1].wait()
    kv_buf[me, :, width:] = activated(1)
    loads[2].wait()
    q_buf[me] = activated(2)
    loads[3].wait()
    pl.semaphore_wait(barrier, n_ctx - 1 + n_dp - 1)

    def kv_copy(peer):
        return ctx_copy("kv", kv_buf.at[me], kv_buf.at[me], peer)

    def q_copy(peer):
        return ctx_copy("q", q_buf.at[me], q_buf.at[me], peer)

    def do_copy(peer):
        return ctx_copy("dout", do_buf.at[me], do_buf.at[me], peer)

    def cot_copy(peer):
        start = pl.multiple_of((peer // f_parts) * c_width, c_width)
        return ctx_copy("cot", cot_ref.at[:, pl.ds(start, c_width)], cot_buf.at[me], peer)

    def mix_copy(peer):
        return ctx_copy("mix", mix_buf.at[me], mix_buf.at[me], peer)

    def tab_copy(peer):
        return ctx_copy("tab", tab_src.at[peer], tab_buf.at[me], peer)

    def gain_copy(peer):
        return ctx_copy("gain", gain_buf.at[me], gain_buf.at[me], peer)

    def wfin_copy(peer):
        return ctx_copy("wfin", wfin_buf.at[me], wfin_buf.at[me], peer)

    def tfin_copy(peer):
        return ctx_copy("tfin", tfin_buf.at[me], tfin_buf.at[me], peer)

    part = lax.rem(me, f_parts)

    def wdp_copy(peer):
        start = pl.multiple_of(peer * dp_rows + part * p_rows, p_rows)
        return dp_copy("wdp", wdp_src.at[pl.ds(start, p_rows)], wdp_buf.at[dpi], peer)

    def tdp_copy(peer):
        return dp_copy("tdp", tdp_src, tdp_buf.at[dpi], peer)

    def gdp_copy(peer):
        return dp_copy("gdp", gdp_src, gdp_buf.at[dpi], peer)

    def for_higher(action):
        @pl.when(core == 0)
        def _():
            action(sibling)

        for d in range(1, chips):
            @pl.when(chip + d < chips)
            def _():
                action(me + 2 * d)

    def for_lower(action):
        @pl.when(core == 1)
        def _():
            action(sibling)

        for d in range(1, chips):
            @pl.when(chip >= d)
            def _():
                action(me - 2 * d)

    def for_partners(action):
        for d in range(1, chips):
            action(ctx_peer(2 * d))
        action(sibling)

    def for_others(action):
        for d in range(1, n_ctx):
            action(ctx_peer(d))

    def for_dp_others(action):
        for d in range(1, n_dp):
            action(dp_peer(d))

    for_higher(lambda p: kv_copy(p).start())
    for_lower(lambda p: q_copy(p).start())
    for_others(lambda p: cot_copy(p).start())
    own_start = pl.multiple_of((me // f_parts) * c_width, c_width)
    cot_buf[me] = cot_ref[:, pl.ds(own_start, c_width)]

    def history(pos):
        bound = jnp.int32(0)
        start = jnp.zeros_like(pos)
        length = jnp.zeros_like(pos)
        for s in range(len_ref.shape[1]):
            here = pos >= bound
            start = jnp.where(here, bound, start)
            length = jnp.where(here, len_ref[0, s], length)
            bound = bound + len_ref[0, s]
        return start, length

    sub = lax.broadcasted_iota(jnp.int32, (rows, rows), 0)
    lane = lax.broadcasted_iota(jnp.int32, (rows, rows), 1)

    def score_parts(s):
        sig = sigmoid(s)
        t = s * sig
        return t, sig + t * (1.0 - sig)

    def key_side_block(i):
        pos_q = i * rows + lane
        pos_k = me * rows + sub
        start, length = history(pos_q)
        allowed = (pos_k >= start) & (pos_k <= pos_q)
        factor = jnp.where(allowed, 1.0 / length.astype(F32), 0.0)
        for h in range(heads):
            cols = slice(h * HD, (h + 1) * HD)
            t, slope = score_parts(dot_nt(kv_buf[me, :, cols], q_buf[i, :, cols]) * scale)
            w_k[i, h] = (t * factor).astype(BF16)
            p_k[i, h] = slope * factor

    for load in loads[4:]:
        load.wait()

    onehot_t = (
        lax.broadcasted_iota(jnp.int32, (ACTIONS, rows), 0) == act_ref[...]
    ).astype(BF16)
    gate_pre = qkvu_ref[:, :width].astype(F32) + dot_tn(onehot_t, table_ref[...])
    gate_sig = sigmoid(gate_pre)
    gate_ref[...] = gate_pre * gate_sig
    gslope_ref[...] = gate_sig * (1.0 + gate_pre * (1.0 - gate_sig))
    gm_ref[...] = dot_nt(cot_ref[...], wout_ref[...])
    key_side_block(me)

    acc[...] = jnp.zeros_like(acc)

    def forward(j):
        pos_q = me * rows + sub
        pos_k = j * rows + lane
        start, length = history(pos_q)
        allowed = (pos_k >= start) & (pos_k <= pos_q)
        factor = jnp.where(allowed, 1.0 / length.astype(F32), 0.0)
        for h in range(heads):
            cols = slice(h * HD, (h + 1) * HD)
            vcols = slice(width + h * HD, width + (h + 1) * HD)
            t, slope = score_parts(dot_nt(q_buf[me, :, cols], kv_buf[j, :, cols]) * scale)
            p_q[j, h] = slope * factor
            acc[:, cols] += dot_nn((t * factor).astype(BF16), kv_buf[j, :, vcols])

    def forward_direct(c, carry):
        forward(2 * c + core)
        return carry

    def forward_relayed(c, carry):
        ctx_arrived("kv", kv_buf, 2 * c + 1 - core)
        forward(2 * c + 1 - core)
        return carry

    lax.fori_loop(chip, chip + 1, forward_direct, 0)

    @pl.when(core == 1)
    def _():
        ctx_arrived("kv", kv_buf, sibling)
        forward(sibling)

    relay("kv", kv_buf, 0, chip)
    lax.fori_loop(0, chip, forward_direct, 0)
    lax.fori_loop(0, chip, forward_relayed, 0)

    attended = acc[...]
    gain = gain_ref[...]
    gate = gate_ref[...]
    centre = attended - jnp.mean(attended, axis=1, keepdims=True)
    inv_std = lax.rsqrt(jnp.mean(centre * centre, axis=1, keepdims=True) + 1e-05)
    normed = centre * inv_std
    mixed = (normed * gain * gate).astype(BF16)
    mix_buf[me] = mixed
    for_partners(lambda p: mix_copy(p).start())
    grad_mixed = gm_ref[...]
    gated = grad_mixed * gate
    pushed = gated * gain
    grad_out = (
        pushed
        - jnp.mean(pushed, axis=1, keepdims=True)
        - normed * jnp.mean(pushed * normed, axis=1, keepdims=True)
    ) * inv_std
    do_buf[me] = grad_out.astype(BF16)
    for_lower(lambda p: do_copy(p).start())
    relay("mix", mix_buf, 0, chip)
    gain_buf[me] = jnp.sum(gated * normed, axis=0, keepdims=True)
    for_others(lambda p: gain_copy(p).start())
    grad_gate = grad_mixed * gain * normed * gslope_ref[...]
    dqkvu_ref[:, :width] = grad_gate.astype(BF16)
    high = grad_gate.astype(BF16)
    low = (grad_gate - high.astype(F32)).astype(BF16)
    table_term = dot_nn(onehot_t, high) + dot_nn(onehot_t, low)
    for s in range(n_ctx):
        tab_src[s] = table_term[s * t_rows : (s + 1) * t_rows]
    for_others(lambda p: tab_copy(p).start())
    tab_buf[me] = tab_src[me]
    relay("q", q_buf, chip + 1, chips)

    out_ref[...] = dot_nn(mixed, wout_ref[...]).astype(BF16)

    acc[...] = jnp.zeros_like(acc)

    def query_grad(step, carry):
        j = me - step
        for h in range(heads):
            cols = slice(h * HD, (h + 1) * HD)
            vcols = slice(width + h * HD, width + (h + 1) * HD)
            prod = dot_nt(do_buf[me, :, cols], kv_buf[j, :, vcols])
            acc[:, cols] += dot_nn((prod * p_q[j, h]).astype(BF16), kv_buf[j, :, cols])
        return carry

    lax.fori_loop(0, me + 1, query_grad, 0)
    q_pre = qkvu_ref[:, 2 * width : 3 * width].astype(F32)
    dqkvu_ref[:, 2 * width : 3 * width] = (acc[...] * scale * silu_slope(q_pre)).astype(BF16)

    @pl.when(core == 0)
    def _():
        ctx_arrived("q", q_buf, sibling)
        key_side_block(sibling)

    def key_side_direct(c, carry):
        key_side_block(2 * c + core)
        return carry

    def key_side_relayed(c, carry):
        ctx_arrived("q", q_buf, 2 * c + 1 - core)
        key_side_block(2 * c + 1 - core)
        return carry

    lax.fori_loop(chip + 1, chips, key_side_direct, 0)
    lax.fori_loop(chip + 1, chips, key_side_relayed, 0)
    relay("mix", mix_buf, chip + 1, chips)

    for_others(lambda p: ctx_arrived("gain", gain_buf, p))
    gain_sum = gain_buf[0]
    for s in range(1, n_ctx):
        gain_sum = gain_sum + gain_buf[s]
    gdp_src[...] = gain_sum
    for_dp_others(lambda p: gdp_copy(p).start())
    gdp_buf[dpi] = gain_sum
    for_others(lambda p: ctx_arrived("tab", tab_buf, p))
    tab_sum = tab_buf[0]
    for s in range(1, n_ctx):
        tab_sum = tab_sum + tab_buf[s]
    tdp_src[...] = tab_sum.astype(tdp_src.dtype)
    for_dp_others(lambda p: tdp_copy(p).start())
    tdp_buf[dpi] = tab_sum.astype(tdp_src.dtype)

    for_others(lambda p: ctx_arrived("cot", cot_buf, p))
    ctx_arrived("mix", mix_buf, sibling)
    for d in range(1, chips):
        ctx_arrived("mix", mix_buf, lax.rem(sibling + 2 * d, n_ctx))
    w_sum = dot_tn(
        mix_buf[...].reshape(n_ctx * rows, width), cot_buf[...].reshape(n_ctx * rows, c_width)
    )
    wdp_src[...] = w_sum.astype(wdp_src.dtype)
    for_dp_others(lambda p: wdp_copy(p).start())
    own_rows = pl.multiple_of(dpi * dp_rows + part * p_rows, p_rows)
    wdp_buf[dpi] = wdp_src[pl.ds(own_rows, p_rows)]

    acc_k[...] = jnp.zeros_like(acc_k)
    acc_v[...] = jnp.zeros_like(acc_v)

    def key_grad(i):
        for h in range(heads):
            cols = slice(h * HD, (h + 1) * HD)
            vcols = slice(width + h * HD, width + (h + 1) * HD)
            grads = do_buf[i, :, cols]
            prod = dot_nt(kv_buf[me, :, vcols], grads)
            acc_k[:, cols] += dot_nn((prod * p_k[i, h]).astype(BF16), q_buf[i, :, cols])
            acc_v[:, cols] += dot_nn(w_k[i, h], grads)

    def key_grad_direct(c, carry):
        key_grad(2 * c + core)
        return carry

    def key_grad_relayed(c, carry):
        ctx_arrived("dout", do_buf, 2 * c + 1 - core)
        key_grad(2 * c + 1 - core)
        return carry

    relay("dout", do_buf, chip + 1, chips)
    lax.fori_loop(chip, chips, key_grad_direct, 0)
    lax.fori_loop(chip + core, chips, key_grad_relayed, 0)
    v_pre = qkvu_ref[:, width : 2 * width].astype(F32)
    dqkvu_ref[:, width : 2 * width] = (acc_v[...] * silu_slope(v_pre)).astype(BF16)
    k_pre = qkvu_ref[:, 3 * width :].astype(F32)
    dqkvu_ref[:, 3 * width :] = (acc_k[...] * scale * silu_slope(k_pre)).astype(BF16)

    for_dp_others(lambda p: dp_arrived("tdp", tdp_buf, p))
    total = tdp_buf[0].astype(F32)
    for s in range(1, n_dp):
        total = total + tdp_buf[s].astype(F32)
    tfin_buf[me] = total
    for_others(lambda p: tfin_copy(p).start())
    for_dp_others(lambda p: dp_arrived("gdp", gdp_buf, p))
    total = gdp_buf[0]
    for s in range(1, n_dp):
        total = total + gdp_buf[s]
    dgain_ref[...] = total
    for_dp_others(lambda p: dp_arrived("wdp", wdp_buf, p))
    total = wdp_buf[0].astype(F32)
    for s in range(1, n_dp):
        total = total + wdp_buf[s].astype(F32)
    wfin_buf[me] = total.astype(wfin_buf.dtype)
    for_others(lambda p: wfin_copy(p).start())
    for_others(lambda p: ctx_arrived("tfin", tfin_buf, p))
    for s in range(n_ctx):
        dtable_ref[s * t_rows : (s + 1) * t_rows] = tfin_buf[s]
    for_others(lambda p: ctx_arrived("wfin", wfin_buf, p))
    for s in range(n_ctx):
        top, left = (s % f_parts) * p_rows, (s // f_parts) * c_width
        dwout_ref[top : top + p_rows, left : left + c_width] = wfin_buf[s].astype(F32)

    for_higher(lambda p: kv_copy(p).wait_send())
    for_lower(lambda p: q_copy(p).wait_send())
    for_lower(lambda p: do_copy(p).wait_send())
    for_partners(lambda p: mix_copy(p).wait_send())
    relay_wait("kv", kv_buf, 0, chip)
    relay_wait("q", q_buf, chip + 1, chips)
    relay_wait("dout", do_buf, chip + 1, chips)
    relay_wait("mix", mix_buf, 0, chip)
    relay_wait("mix", mix_buf, chip + 1, chips)
    for copy in (cot_copy, tab_copy, gain_copy, wfin_copy, tfin_copy):
        for_others(lambda p: copy(p).wait_send())
    for copy in (wdp_copy, tdp_copy, gdp_copy):
        for_dp_others(lambda p: copy(p).wait_send())


def store_kernel(*refs):
    sems = refs[10]
    stores = [pltpu.make_async_copy(refs[n], refs[5 + n], sems.at[n]) for n in range(5)]
    for store in stores:
        store.start()
    for store in stores:
        store.wait()


def on_device(n_ctx, n_dp, qkvu, actions, lengths, action_table, gain, w_out, cotangent):
    rows = qkvu.shape[0]
    width, model = w_out.shape
    heads = width // HD
    c_parts = min(n_ctx, model // 128)
    f_parts = n_ctx // c_parts
    c_width = model // c_parts
    dp_rows = width // n_dp
    p_rows = dp_rows // f_parts
    t_rows = ACTIONS // n_ctx
    w_kind = BF16 if p_rows % 16 == 0 else F32
    t_kind = BF16 if t_rows % 16 == 0 else F32
    vmem = pl.BlockSpec(memory_space=pltpu.VMEM)
    outs = pl.pallas_call(
        functools.partial(layer_kernel, n_ctx, n_dp, f_parts),
        out_shape=(
            jax.ShapeDtypeStruct((rows, model), BF16),
            jax.ShapeDtypeStruct((rows, 4 * width), BF16),
            jax.ShapeDtypeStruct((dp_rows, model), F32),
            jax.ShapeDtypeStruct((ACTIONS, width), F32),
            jax.ShapeDtypeStruct((1, width), F32),
        ),
        in_specs=[pl.BlockSpec(memory_space=pltpu.HBM)] * 7,
        out_specs=(vmem,) * 5,
        scratch_shapes=[
            pltpu.VMEM((n_ctx, rows, 2 * width), BF16),
            pltpu.VMEM((n_ctx, rows, width), BF16),
            pltpu.VMEM((n_ctx, rows, c_width), BF16),
            pltpu.VMEM((n_ctx, rows, width), BF16),
            pltpu.VMEM((n_ctx, rows, width), BF16),
            pltpu.VMEM((n_ctx, t_rows, width), F32),
            pltpu.VMEM((n_ctx, t_rows, width), F32),
            pltpu.VMEM((n_ctx, 1, width), F32),
            pltpu.VMEM((width, c_width), w_kind),
            pltpu.VMEM((n_dp, p_rows, c_width), w_kind),
            pltpu.VMEM((t_rows, width), t_kind),
            pltpu.VMEM((n_dp, t_rows, width), t_kind),
            pltpu.VMEM((1, width), F32),
            pltpu.VMEM((n_dp, 1, width), F32),
            pltpu.VMEM((n_ctx, p_rows, c_width), w_kind),
            pltpu.VMEM((n_ctx, t_rows, width), F32),
            pltpu.VMEM((n_ctx, heads, rows, rows), F32),
            pltpu.VMEM((n_ctx, heads, rows, rows), BF16),
            pltpu.VMEM((n_ctx, heads, rows, rows), F32),
            pltpu.VMEM((rows, width), F32),
            pltpu.VMEM((rows, width), F32),
            pltpu.VMEM((rows, width), F32),
            pltpu.VMEM((rows, width), F32),
            pltpu.VMEM((rows, width), F32),
            pltpu.VMEM((rows, width), F32),
            pltpu.VMEM((rows, 4 * width), BF16),
            pltpu.VMEM((1, rows), jnp.int32),
            pltpu.SMEM(lengths.shape, jnp.int32),
            pltpu.VMEM(action_table.shape, BF16),
            pltpu.VMEM((1, width), F32),
            pltpu.VMEM((width, model), BF16),
            pltpu.VMEM((rows, model), BF16),
            pltpu.SemaphoreType.DMA((len(CTX_KINDS), n_ctx)),
            pltpu.SemaphoreType.DMA((len(CTX_KINDS), n_ctx)),
            pltpu.SemaphoreType.DMA((len(CTX_KINDS), n_ctx)),
            pltpu.SemaphoreType.DMA((len(DP_KINDS), n_dp)),
            pltpu.SemaphoreType.DMA((len(DP_KINDS), n_dp)),
            pltpu.SemaphoreType.DMA((10,)),
        ],
        compiler_params=pltpu.CompilerParams(
            collective_id=0, has_side_effects=True, vmem_limit_bytes=64 * 1024 * 1024
        ),
        name="attention_layer",
    )(
        qkvu, actions.reshape(1, rows), lengths, action_table,
        gain.reshape(1, width), w_out, cotangent,
    )
    output, d_qkvu, d_wout, d_table, d_gain = pl.pallas_call(
        store_kernel,
        out_shape=[jax.ShapeDtypeStruct(o.shape, o.dtype) for o in outs],
        in_specs=[vmem] * 5,
        out_specs=[pl.BlockSpec(memory_space=pl.ANY)] * 5,
        scratch_shapes=[pltpu.SemaphoreType.DMA((5,))],
        compiler_params=pltpu.CompilerParams(vmem_limit_bytes=64 * 1024 * 1024),
        name="store_results",
    )(*outs)
    return output, d_qkvu, d_wout, d_table, d_gain.reshape(width)


def solution(mesh):
    both = P(("dp", "ctx"), None)
    return jax.shard_map(
        functools.partial(on_device, mesh.shape["ctx"], mesh.shape["dp"]),
        mesh=mesh,
        in_specs=(both, P(("dp", "ctx")), P("dp", None), P(), P(), P(), both),
        out_specs=(both, both, P("dp", None), P(), P()),
        check_vma=False,
    )
```

```python
import functools

import jax
import jax.numpy as jnp
from jax import lax
from jax.experimental import pallas as pl
from jax.experimental.pallas import tpu as pltpu
from jax.sharding import PartitionSpec as P

HD = 128
ACTIONS = 64
F32 = jnp.float32
BF16 = jnp.bfloat16
CTX_KINDS = ("kv", "q", "cot", "mix", "dout", "tab", "gain", "wfin", "tfin")
DP_KINDS = ("wdp", "tdp", "gdp")


def sigmoid(x):
    return 0.5 * jnp.tanh(0.5 * x) + 0.5


def silu_slope(x):
    sig = sigmoid(x)
    return sig * (1.0 + x * (1.0 - sig))


def dot_nn(a, b):
    return lax.dot_general(a, b, (((1,), (0,)), ((), ())), preferred_element_type=F32)


def dot_nt(a, b):
    return lax.dot_general(a, b, (((1,), (1,)), ((), ())), preferred_element_type=F32)


def dot_tn(a, b):
    return lax.dot_general(a, b, (((0,), (0,)), ((), ())), preferred_element_type=F32)


def layer_kernel(
    n_ctx, n_dp, f_parts,
    qkvu_in, act_in, len_in, table_in, gain_in, wout_in, cot_in,
    out_ref, dqkvu_ref, dwout_ref, dtable_ref, dgain_ref,
    kv_buf, q_buf, cot_buf, mix_buf, do_buf, tab_src, tab_buf, gain_buf,
    wdp_src, wdp_buf, tdp_src, tdp_buf, gdp_src, gdp_buf, wfin_buf, tfin_buf,
    p_q, w_k, p_k, acc, acc_k, acc_v, gm_ref, gate_ref, gslope_ref,
    qkvu_ref, act_ref, len_ref, table_ref, gain_ref, wout_ref, cot_ref,
    ctx_send, ctx_recv, relay_send, dp_send, dp_recv, load_sem,
):
    me = lax.axis_index("ctx")
    dpi = lax.axis_index("dp")
    rows = qkvu_ref.shape[0]
    width = wout_ref.shape[0]
    heads = width // HD
    scale = HD ** (-0.5)
    c_width = cot_buf.shape[2]
    dp_rows = dwout_ref.shape[0]
    p_rows = dp_rows // f_parts
    t_rows = tab_buf.shape[1]

    def ctx_copy(kind, src, dst, peer):
        k = CTX_KINDS.index(kind)
        return pltpu.make_async_remote_copy(
            src_ref=src, dst_ref=dst,
            send_sem=ctx_send.at[k, peer], recv_sem=ctx_recv.at[k, me],
            device_id={"ctx": peer}, device_id_type=pl.DeviceIdType.MESH,
        )

    def ctx_arrived(kind, buf, source):
        k = CTX_KINDS.index(kind)
        pltpu.make_async_remote_copy(
            src_ref=buf.at[source], dst_ref=buf.at[source],
            send_sem=ctx_send.at[k, source], recv_sem=ctx_recv.at[k, source],
            device_id={"ctx": source}, device_id_type=pl.DeviceIdType.MESH,
        ).wait_recv()

    def dp_copy(kind, src, dst, peer):
        k = DP_KINDS.index(kind)
        return pltpu.make_async_remote_copy(
            src_ref=src, dst_ref=dst,
            send_sem=dp_send.at[k, peer], recv_sem=dp_recv.at[k, dpi],
            device_id={"dp": peer}, device_id_type=pl.DeviceIdType.MESH,
        )

    def dp_arrived(kind, buf, source):
        k = DP_KINDS.index(kind)
        pltpu.make_async_remote_copy(
            src_ref=buf.at[source], dst_ref=buf.at[source],
            send_sem=dp_send.at[k, source], recv_sem=dp_recv.at[k, source],
            device_id={"dp": source}, device_id_type=pl.DeviceIdType.MESH,
        ).wait_recv()

    def ctx_peer(d):
        return lax.rem(me + d, n_ctx)

    def dp_peer(d):
        return lax.rem(dpi + d, n_dp)

    core = lax.rem(me, 2)
    chip = me // 2
    chips = n_ctx // 2
    sibling = me + 1 - 2 * core

    def relay_copy(kind, buf, slot):
        k = CTX_KINDS.index(kind)
        return pltpu.make_async_remote_copy(
            src_ref=buf.at[slot], dst_ref=buf.at[slot],
            send_sem=relay_send.at[k, slot], recv_sem=ctx_recv.at[k, slot],
            device_id={"ctx": sibling}, device_id_type=pl.DeviceIdType.MESH,
        )

    def relay(kind, buf, low, high):
        def step(c, carry):
            ctx_arrived(kind, buf, 2 * c + core)
            relay_copy(kind, buf, 2 * c + core).start()
            return carry

        lax.fori_loop(low, high, step, 0)

    def relay_wait(kind, buf, low, high):
        def step(c, carry):
            relay_copy(kind, buf, 2 * c + core).wait_send()
            return carry

        lax.fori_loop(low, high, step, 0)

    barrier = pltpu.get_barrier_semaphore()
    for d in range(1, n_ctx):
        pl.semaphore_signal(
            barrier, inc=1, device_id={"ctx": ctx_peer(d)}, device_id_type=pl.DeviceIdType.MESH
        )
    for d in range(1, n_dp):
        pl.semaphore_signal(
            barrier, inc=1, device_id={"dp": dp_peer(d)}, device_id_type=pl.DeviceIdType.MESH
        )

    qkvu_cols = [slice(b * width, (b + 1) * width) for b in range(4)]
    loads = [
        pltpu.make_async_copy(source, target, load_sem.at[n])
        for n, (source, target) in enumerate(
            [(qkvu_in.at[:, qkvu_cols[b]], qkvu_ref.at[:, qkvu_cols[b]]) for b in (3, 1, 2)]
            + [(cot_in, cot_ref), (wout_in, wout_ref), (len_in, len_ref)]
            + [(qkvu_in.at[:, qkvu_cols[0]], qkvu_ref.at[:, qkvu_cols[0]])]
            + [(table_in, table_ref), (act_in, act_ref), (gain_in, gain_ref)]
        )
    ]
    for load in loads:
        load.start()

    def activated(block):
        x = qkvu_ref[:, block * width : (block + 1) * width].astype(F32)
        return (x * sigmoid(x)).astype(BF16)

    loads[0].wait()
    kv_buf[me, :, :width] = activated(3)
    loads[1].wait()
    kv_buf[me, :, width:] = activated(1)
    loads[2].wait()
    q_buf[me] = activated(2)
    loads[3].wait()
    pl.semaphore_wait(barrier, n_ctx - 1 + n_dp - 1)

    def kv_copy(peer):
        return ctx_copy("kv", kv_buf.at[me], kv_buf.at[me], peer)

    def q_copy(peer):
        return ctx_copy("q", q_buf.at[me], q_buf.at[me], peer)

    def do_copy(peer):
        return ctx_copy("dout", do_buf.at[me], do_buf.at[me], peer)

    def cot_copy(peer):
        start = pl.multiple_of((peer // f_parts) * c_width, c_width)
        return ctx_copy("cot", cot_ref.at[:, pl.ds(start, c_width)], cot_buf.at[me], peer)

    def mix_copy(peer):
        return ctx_copy("mix", mix_buf.at[me], mix_buf.at[me], peer)

    def tab_copy(peer):
        return ctx_copy("tab", tab_src.at[peer], tab_buf.at[me], peer)

    def gain_copy(peer):
        return ctx_copy("gain", gain_buf.at[me], gain_buf.at[me], peer)

    def wfin_copy(peer):
        return ctx_copy("wfin", wfin_buf.at[me], wfin_buf.at[me], peer)

    def tfin_copy(peer):
        return ctx_copy("tfin", tfin_buf.at[me], tfin_buf.at[me], peer)

    part = lax.rem(me, f_parts)

    def wdp_copy(peer):
        start = pl.multiple_of(peer * dp_rows + part * p_rows, p_rows)
        return dp_copy("wdp", wdp_src.at[pl.ds(start, p_rows)], wdp_buf.at[dpi], peer)

    def tdp_copy(peer):
        return dp_copy("tdp", tdp_src, tdp_buf.at[dpi], peer)

    def gdp_copy(peer):
        return dp_copy("gdp", gdp_src, gdp_buf.at[dpi], peer)

    def for_higher(action):
        for d in range(1, chips):
            @pl.when(chip + d < chips)
            def _():
                action(me + 2 * d)

        @pl.when(core == 0)
        def _():
            action(sibling)

    def for_lower(action):
        for d in range(1, chips):
            @pl.when(chip >= d)
            def _():
                action(me - 2 * d)

        @pl.when(core == 1)
        def _():
            action(sibling)

    def for_partners(action):
        for d in range(1, chips):
            action(ctx_peer(2 * d))
        action(sibling)

    def for_others(action):
        for d in range(1, n_ctx):
            action(ctx_peer(d))

    def for_dp_others(action):
        for d in range(1, n_dp):
            action(dp_peer(d))

    for_higher(lambda p: kv_copy(p).start())
    for_lower(lambda p: q_copy(p).start())
    for_others(lambda p: cot_copy(p).start())
    own_start = pl.multiple_of((me // f_parts) * c_width, c_width)
    cot_buf[me] = cot_ref[:, pl.ds(own_start, c_width)]

    def history(pos):
        bound = jnp.int32(0)
        start = jnp.zeros_like(pos)
        length = jnp.zeros_like(pos)
        for s in range(len_ref.shape[1]):
            here = pos >= bound
            start = jnp.where(here, bound, start)
            length = jnp.where(here, len_ref[0, s], length)
            bound = bound + len_ref[0, s]
        return start, length

    sub = lax.broadcasted_iota(jnp.int32, (rows, rows), 0)
    lane = lax.broadcasted_iota(jnp.int32, (rows, rows), 1)

    def score_parts(s):
        sig = sigmoid(s)
        t = s * sig
        return t, sig + t * (1.0 - sig)

    def key_side_block(i):
        pos_q = i * rows + lane
        pos_k = me * rows + sub
        start, length = history(pos_q)
        allowed = (pos_k >= start) & (pos_k <= pos_q)
        factor = jnp.where(allowed, 1.0 / length.astype(F32), 0.0)
        for h in range(heads):
            cols = slice(h * HD, (h + 1) * HD)
            t, slope = score_parts(dot_nt(kv_buf[me, :, cols], q_buf[i, :, cols]) * scale)
            w_k[i, h] = (t * factor).astype(BF16)
            p_k[i, h] = slope * factor

    for load in loads[4:]:
        load.wait()

    onehot_t = (
        lax.broadcasted_iota(jnp.int32, (ACTIONS, rows), 0) == act_ref[...]
    ).astype(BF16)
    gate_pre = qkvu_ref[:, :width].astype(F32) + dot_tn(onehot_t, table_ref[...])
    gate_sig = sigmoid(gate_pre)
    gate_ref[...] = gate_pre * gate_sig
    gslope_ref[...] = gate_sig * (1.0 + gate_pre * (1.0 - gate_sig))
    gm_ref[...] = dot_nt(cot_ref[...], wout_ref[...])
    key_side_block(me)

    acc[...] = jnp.zeros_like(acc)

    def forward(j):
        pos_q = me * rows + sub
        pos_k = j * rows + lane
        start, length = history(pos_q)
        allowed = (pos_k >= start) & (pos_k <= pos_q)
        factor = jnp.where(allowed, 1.0 / length.astype(F32), 0.0)
        for h in range(heads):
            cols = slice(h * HD, (h + 1) * HD)
            vcols = slice(width + h * HD, width + (h + 1) * HD)
            t, slope = score_parts(dot_nt(q_buf[me, :, cols], kv_buf[j, :, cols]) * scale)
            p_q[j, h] = slope * factor
            acc[:, cols] += dot_nn((t * factor).astype(BF16), kv_buf[j, :, vcols])

    def forward_direct(c, carry):
        forward(2 * c + core)
        return carry

    def forward_relayed(c, carry):
        ctx_arrived("kv", kv_buf, 2 * c + 1 - core)
        forward(2 * c + 1 - core)
        return carry

    lax.fori_loop(chip, chip + 1, forward_direct, 0)

    @pl.when(core == 1)
    def _():
        ctx_arrived("kv", kv_buf, sibling)
        forward(sibling)

    relay("kv", kv_buf, 0, chip)
    lax.fori_loop(0, chip, forward_direct, 0)
    lax.fori_loop(0, chip, forward_relayed, 0)

    attended = acc[...]
    gain = gain_ref[...]
    gate = gate_ref[...]
    centre = attended - jnp.mean(attended, axis=1, keepdims=True)
    inv_std = lax.rsqrt(jnp.mean(centre * centre, axis=1, keepdims=True) + 1e-05)
    normed = centre * inv_std
    mixed = (normed * gain * gate).astype(BF16)
    mix_buf[me] = mixed
    for_partners(lambda p: mix_copy(p).start())
    grad_mixed = gm_ref[...]
    gated = grad_mixed * gate
    pushed = gated * gain
    grad_out = (
        pushed
        - jnp.mean(pushed, axis=1, keepdims=True)
        - normed * jnp.mean(pushed * normed, axis=1, keepdims=True)
    ) * inv_std
    do_buf[me] = grad_out.astype(BF16)
    for_lower(lambda p: do_copy(p).start())
    relay("mix", mix_buf, 0, chip)
    gain_buf[me] = jnp.sum(gated * normed, axis=0, keepdims=True)
    for_others(lambda p: gain_copy(p).start())
    grad_gate = grad_mixed * gain * normed * gslope_ref[...]
    dqkvu_ref[:, :width] = grad_gate.astype(BF16)
    high = grad_gate.astype(BF16)
    low = (grad_gate - high.astype(F32)).astype(BF16)
    table_term = dot_nn(onehot_t, high) + dot_nn(onehot_t, low)
    for s in range(n_ctx):
        tab_src[s] = table_term[s * t_rows : (s + 1) * t_rows]
    for_others(lambda p: tab_copy(p).start())
    tab_buf[me] = tab_src[me]
    relay("q", q_buf, chip + 1, chips)

    def project():
        for_others(lambda p: ctx_arrived("cot", cot_buf, p))
        ctx_arrived("mix", mix_buf, sibling)
        for d in range(1, chips):
            ctx_arrived("mix", mix_buf, lax.rem(sibling + 2 * d, n_ctx))
        w_sum = dot_tn(
            mix_buf[...].reshape(n_ctx * rows, width), cot_buf[...].reshape(n_ctx * rows, c_width)
        )
        wdp_src[...] = w_sum.astype(wdp_src.dtype)
        for_dp_others(lambda p: wdp_copy(p).start())
        own_rows = pl.multiple_of(dpi * dp_rows + part * p_rows, p_rows)
        wdp_buf[dpi] = wdp_src[pl.ds(own_rows, p_rows)]

    @pl.when(chip == chips - 1)
    def _():
        project()

    out_ref[...] = dot_nn(mixed, wout_ref[...]).astype(BF16)

    acc[...] = jnp.zeros_like(acc)

    def query_grad(step, carry):
        j = me - step
        for h in range(heads):
            cols = slice(h * HD, (h + 1) * HD)
            vcols = slice(width + h * HD, width + (h + 1) * HD)
            prod = dot_nt(do_buf[me, :, cols], kv_buf[j, :, vcols])
            acc[:, cols] += dot_nn((prod * p_q[j, h]).astype(BF16), kv_buf[j, :, cols])
        return carry

    lax.fori_loop(0, me + 1, query_grad, 0)
    q_pre = qkvu_ref[:, 2 * width : 3 * width].astype(F32)
    dqkvu_ref[:, 2 * width : 3 * width] = (acc[...] * scale * silu_slope(q_pre)).astype(BF16)

    @pl.when(core == 0)
    def _():
        ctx_arrived("q", q_buf, sibling)
        key_side_block(sibling)

    def key_side_direct(c, carry):
        key_side_block(2 * c + core)
        return carry

    def key_side_relayed(c, carry):
        ctx_arrived("q", q_buf, 2 * c + 1 - core)
        key_side_block(2 * c + 1 - core)
        return carry

    lax.fori_loop(chip + 1, chips, key_side_direct, 0)
    lax.fori_loop(chip + 1, chips, key_side_relayed, 0)
    relay("mix", mix_buf, chip + 1, chips)

    @pl.when(chip < chips - 1)
    def _():
        project()

    for_others(lambda p: ctx_arrived("gain", gain_buf, p))
    gain_sum = gain_buf[0]
    for s in range(1, n_ctx):
        gain_sum = gain_sum + gain_buf[s]
    gdp_src[...] = gain_sum
    for_dp_others(lambda p: gdp_copy(p).start())
    gdp_buf[dpi] = gain_sum
    for_others(lambda p: ctx_arrived("tab", tab_buf, p))
    tab_sum = tab_buf[0]
    for s in range(1, n_ctx):
        tab_sum = tab_sum + tab_buf[s]
    tdp_src[...] = tab_sum.astype(tdp_src.dtype)
    for_dp_others(lambda p: tdp_copy(p).start())
    tdp_buf[dpi] = tab_sum.astype(tdp_src.dtype)

    acc_k[...] = jnp.zeros_like(acc_k)
    acc_v[...] = jnp.zeros_like(acc_v)

    def key_grad(i):
        for h in range(heads):
            cols = slice(h * HD, (h + 1) * HD)
            vcols = slice(width + h * HD, width + (h + 1) * HD)
            grads = do_buf[i, :, cols]
            prod = dot_nt(kv_buf[me, :, vcols], grads)
            acc_k[:, cols] += dot_nn((prod * p_k[i, h]).astype(BF16), q_buf[i, :, cols])
            acc_v[:, cols] += dot_nn(w_k[i, h], grads)

    def key_grad_direct(c, carry):
        key_grad(2 * c + core)
        return carry

    def key_grad_relayed(c, carry):
        ctx_arrived("dout", do_buf, 2 * c + 1 - core)
        key_grad(2 * c + 1 - core)
        return carry

    relay("dout", do_buf, chip + 1, chips)
    lax.fori_loop(chip, chips, key_grad_direct, 0)
    lax.fori_loop(chip + core, chips, key_grad_relayed, 0)
    v_pre = qkvu_ref[:, width : 2 * width].astype(F32)
    dqkvu_ref[:, width : 2 * width] = (acc_v[...] * silu_slope(v_pre)).astype(BF16)
    k_pre = qkvu_ref[:, 3 * width :].astype(F32)
    dqkvu_ref[:, 3 * width :] = (acc_k[...] * scale * silu_slope(k_pre)).astype(BF16)

    for_dp_others(lambda p: dp_arrived("tdp", tdp_buf, p))
    total = tdp_buf[0].astype(F32)
    for s in range(1, n_dp):
        total = total + tdp_buf[s].astype(F32)
    tfin_buf[me] = total
    for_others(lambda p: tfin_copy(p).start())
    for_dp_others(lambda p: dp_arrived("gdp", gdp_buf, p))
    total = gdp_buf[0]
    for s in range(1, n_dp):
        total = total + gdp_buf[s]
    dgain_ref[...] = total
    for_dp_others(lambda p: dp_arrived("wdp", wdp_buf, p))
    total = wdp_buf[0].astype(F32)
    for s in range(1, n_dp):
        total = total + wdp_buf[s].astype(F32)
    wfin_buf[me] = total.astype(wfin_buf.dtype)
    for_others(lambda p: wfin_copy(p).start())
    for_others(lambda p: ctx_arrived("tfin", tfin_buf, p))
    for s in range(n_ctx):
        dtable_ref[s * t_rows : (s + 1) * t_rows] = tfin_buf[s]
    for_others(lambda p: ctx_arrived("wfin", wfin_buf, p))
    for s in range(n_ctx):
        top, left = (s % f_parts) * p_rows, (s // f_parts) * c_width
        dwout_ref[top : top + p_rows, left : left + c_width] = wfin_buf[s].astype(F32)

    for_higher(lambda p: kv_copy(p).wait_send())
    for_lower(lambda p: q_copy(p).wait_send())
    for_lower(lambda p: do_copy(p).wait_send())
    for_partners(lambda p: mix_copy(p).wait_send())
    relay_wait("kv", kv_buf, 0, chip)
    relay_wait("q", q_buf, chip + 1, chips)
    relay_wait("dout", do_buf, chip + 1, chips)
    relay_wait("mix", mix_buf, 0, chip)
    relay_wait("mix", mix_buf, chip + 1, chips)
    for copy in (cot_copy, tab_copy, gain_copy, wfin_copy, tfin_copy):
        for_others(lambda p: copy(p).wait_send())
    for copy in (wdp_copy, tdp_copy, gdp_copy):
        for_dp_others(lambda p: copy(p).wait_send())


def store_kernel(*refs):
    sems = refs[10]
    stores = [pltpu.make_async_copy(refs[n], refs[5 + n], sems.at[n]) for n in range(5)]
    for store in stores:
        store.start()
    for store in stores:
        store.wait()


def on_device(n_ctx, n_dp, qkvu, actions, lengths, action_table, gain, w_out, cotangent):
    rows = qkvu.shape[0]
    width, model = w_out.shape
    heads = width // HD
    c_parts = min(n_ctx, model // 128)
    f_parts = n_ctx // c_parts
    c_width = model // c_parts
    dp_rows = width // n_dp
    p_rows = dp_rows // f_parts
    t_rows = ACTIONS // n_ctx
    w_kind = BF16 if p_rows % 16 == 0 else F32
    t_kind = BF16 if t_rows % 16 == 0 else F32
    vmem = pl.BlockSpec(memory_space=pltpu.VMEM)
    outs = pl.pallas_call(
        functools.partial(layer_kernel, n_ctx, n_dp, f_parts),
        out_shape=(
            jax.ShapeDtypeStruct((rows, model), BF16),
            jax.ShapeDtypeStruct((rows, 4 * width), BF16),
            jax.ShapeDtypeStruct((dp_rows, model), F32),
            jax.ShapeDtypeStruct((ACTIONS, width), F32),
            jax.ShapeDtypeStruct((1, width), F32),
        ),
        in_specs=[pl.BlockSpec(memory_space=pltpu.HBM)] * 7,
        out_specs=(vmem,) * 5,
        scratch_shapes=[
            pltpu.VMEM((n_ctx, rows, 2 * width), BF16),
            pltpu.VMEM((n_ctx, rows, width), BF16),
            pltpu.VMEM((n_ctx, rows, c_width), BF16),
            pltpu.VMEM((n_ctx, rows, width), BF16),
            pltpu.VMEM((n_ctx, rows, width), BF16),
            pltpu.VMEM((n_ctx, t_rows, width), F32),
            pltpu.VMEM((n_ctx, t_rows, width), F32),
            pltpu.VMEM((n_ctx, 1, width), F32),
            pltpu.VMEM((width, c_width), w_kind),
            pltpu.VMEM((n_dp, p_rows, c_width), w_kind),
            pltpu.VMEM((t_rows, width), t_kind),
            pltpu.VMEM((n_dp, t_rows, width), t_kind),
            pltpu.VMEM((1, width), F32),
            pltpu.VMEM((n_dp, 1, width), F32),
            pltpu.VMEM((n_ctx, p_rows, c_width), w_kind),
            pltpu.VMEM((n_ctx, t_rows, width), F32),
            pltpu.VMEM((n_ctx, heads, rows, rows), F32),
            pltpu.VMEM((n_ctx, heads, rows, rows), BF16),
            pltpu.VMEM((n_ctx, heads, rows, rows), F32),
            pltpu.VMEM((rows, width), F32),
            pltpu.VMEM((rows, width), F32),
            pltpu.VMEM((rows, width), F32),
            pltpu.VMEM((rows, width), F32),
            pltpu.VMEM((rows, width), F32),
            pltpu.VMEM((rows, width), F32),
            pltpu.VMEM((rows, 4 * width), BF16),
            pltpu.VMEM((1, rows), jnp.int32),
            pltpu.SMEM(lengths.shape, jnp.int32),
            pltpu.VMEM(action_table.shape, BF16),
            pltpu.VMEM((1, width), F32),
            pltpu.VMEM((width, model), BF16),
            pltpu.VMEM((rows, model), BF16),
            pltpu.SemaphoreType.DMA((len(CTX_KINDS), n_ctx)),
            pltpu.SemaphoreType.DMA((len(CTX_KINDS), n_ctx)),
            pltpu.SemaphoreType.DMA((len(CTX_KINDS), n_ctx)),
            pltpu.SemaphoreType.DMA((len(DP_KINDS), n_dp)),
            pltpu.SemaphoreType.DMA((len(DP_KINDS), n_dp)),
            pltpu.SemaphoreType.DMA((10,)),
        ],
        compiler_params=pltpu.CompilerParams(
            collective_id=0, has_side_effects=True, vmem_limit_bytes=64 * 1024 * 1024
        ),
        name="attention_layer",
    )(
        qkvu, actions.reshape(1, rows), lengths, action_table,
        gain.reshape(1, width), w_out, cotangent,
    )
    output, d_qkvu, d_wout, d_table, d_gain = pl.pallas_call(
        store_kernel,
        out_shape=[jax.ShapeDtypeStruct(o.shape, o.dtype) for o in outs],
        in_specs=[vmem] * 5,
        out_specs=[pl.BlockSpec(memory_space=pl.ANY)] * 5,
        scratch_shapes=[pltpu.SemaphoreType.DMA((5,))],
        compiler_params=pltpu.CompilerParams(vmem_limit_bytes=64 * 1024 * 1024),
        name="store_results",
    )(*outs)
    return output, d_qkvu, d_wout, d_table, d_gain.reshape(width)


def solution(mesh):
    both = P(("dp", "ctx"), None)
    return jax.shard_map(
        functools.partial(on_device, mesh.shape["ctx"], mesh.shape["dp"]),
        mesh=mesh,
        in_specs=(both, P(("dp", "ctx")), P("dp", None), P(), P(), P(), both),
        out_specs=(both, both, P("dp", None), P(), P()),
        check_vma=False,
    )
```
